32 devices in a mesh: ens: 2 (over y), band: 16 (over z, x, core).
Axes of the slice: x: 2, y: 2, z: 4, core: 2. Of those that a mesh axis runs over, the one named last changes fastest.
Arguments:
- grid_in: bfloat16 [32768, 256], P(('ens', 'band')), parts along dimension 0, may hold values from -6 to 6
- mesh_state: bfloat16 [8192, 512], P('band'), may hold values from -6 to 6
- enc_owner: int32 [16384, 1], P('band'), may hold values from 0 to 15; in each aligned block of 1024 rows (0 to 1023, 1024 to 2047, ...) at most 128 rows name the same one
- enc_slot: int32 [16384, 1], P('band'), may hold values from 0 to 511
- dec_owner: int32 [16384, 1], P('band'), may hold values from 0 to 15; in each aligned block of 1024 rows (0 to 1023, 1024 to 2047, ...) at most 128 rows name the same one
- dec_slot: int32 [16384, 3], P('band'), may hold values from 0 to 511
- dec_weight: float32 [16384, 3], P('band'), may hold values from 0.2 to 1
- att_list: int32 [64, 4], P('band'), may hold values from 0 to 7, all different within a row
- w_embed: bfloat16 [256, 512], replicated, may hold values from -0.375 to 0.375
- w_message: bfloat16 [512, 512], replicated, may hold values from -0.25 to 0.25
- norm_gain: float32 [3, 512], replicated, may hold values from 0.1 to 1.9
- w_qkv: bfloat16 [1, 512, 1536], replicated, may hold values from -6 to 6
- w_out: bfloat16 [1, 512, 512], replicated, may hold values from -0.25 to 0.25
- w_up: bfloat16 [1, 512, 2048], replicated, may hold values from -0.25 to 0.25
- w_down: bfloat16 [1, 2048, 512], replicated, may hold values from -0.125 to 0.125
- w_dec1: bfloat16 [512, 512], replicated, may hold values from -0.25 to 0.25
- w_dec2: bfloat16 [512, 84], replicated, may hold values from -0.25 to 0.25
Outputs:
- denoised: bfloat16 [84, 32768], P(None, ('ens', 'band')), parts along dimension 1
The draws below stay inside these ranges and needn't reach their ends.
There are 2 independent parts, one for each index of `ens`. The reference program is written for one: setup_inputs(seed, part) draws one part's arguments, and reference() takes and returns one part's arrays. A program takes and returns all parts, laid end to end along the dimension named above; an argument that names none is the same for every part. Nothing has to cross between parts.
Inputs may be any that keep to these rules, and one draw needn't show every extreme that they name: `enc_owner`: in the rows of one band (aligned blocks of 1024 rows) no mesh shard is named by more than 128 rows. `dec_owner`: in the rows of one band (aligned blocks of 1024 rows) no mesh shard is named by more than 128 rows. `att_list`: each row names 4 different window blocks.
All inputs are finite; a program needn't handle non-finite values.
Results may differ from the reference program's by a relative error of at most 0.014.
Values may be sent and summed in bfloat16 or wider, within the bound.
No kernel may reach another device: no remote copies, remote signals or barrier semaphores. Data moves between devices by JAX's collectives and lax.ppermute only.
A program may use at most 128 MiB of HBM per device.

```python
import math
import jax
import jax.numpy as jnp
import numpy as np
from jax import lax

D = 512
HEADS = 4
FF = 2048
C_OUT = 84
C_IN = 256
GRID_DEV = 1024
BLK = 128
BLK_DEV = 4
NB = 4
LAYERS = 1
HD = 128
MESH_DEV = 512
GRID = 16384
MESH = 8192
MESH_BLOCKS = 64
CAP = 128
N_BAND = 16


def draw_w_qkv(key, part):
    key = jax.random.fold_in(key, 11)
    standard = jax.random.truncated_normal(key, -4.0, 4.0, (LAYERS, D, 3 * D), jnp.float32) * D ** (-0.5)
    return standard.astype(jnp.bfloat16)


def with_ends(values, stream_key, low, top_value):
    dims = values.shape
    place = [jax.random.randint(jax.random.fold_in(stream_key, axis), (), 0, dims[axis]) for axis in range(len(dims))]
    values = values.at[tuple(place)].set(low)
    longest = dims.index(max(dims))
    place[longest] = (place[longest] + 1) % dims[longest]
    return values.at[tuple(place)].set(top_value)


def levels(rng, dims, shards, least, high):
    def one(axis_at, shards_of):
        heights = jax.random.uniform(jax.random.fold_in(jax.random.fold_in(rng, 6), axis_at), (shards_of,), jnp.float32, least / len(shards), high / len(shards))
        return jnp.repeat(jnp.exp(heights), dims[axis_at] // shards_of).reshape((-1,) + (1,) * (len(dims) - axis_at - 1))

    loudness = one(*shards[0])
    for cut in shards[1:]:
        loudness = loudness * one(*cut)
    return loudness


def choose_distinct(stream_key, rows, number_of, top, lift):
    sequence = jax.random.permutation(jax.random.fold_in(stream_key, 1), number_of)
    favour = sequence
    for power in range(3):
        favour = favour * favour // number_of
    favour = favour * lift // number_of
    lots = jax.random.randint(jax.random.fold_in(stream_key, 2), (rows, number_of), 0, 4096) + favour
    sure = jax.random.permutation(jax.random.fold_in(stream_key, 3), rows)[jnp.arange(number_of) % rows]
    lots = jnp.where(jnp.arange(rows)[:, None] == sure[None, :], 1 << 14, lots)
    priority = lots * number_of + jnp.arange(number_of)
    return lax.top_k(priority.astype(jnp.int32), top)[1].astype(jnp.int32)


def shared_out(key, own, number, rows, number_of, top, reach, slope):
    sequence = jax.random.permutation(key, number_of)
    packed, usual = shares(number_of, rows * top, reach, slope, True), shares(number_of, rows * top, reach, slope, False)
    places = jnp.arange(number_of)

    def named(tallies, rotation):
        used = int((tallies > 0).sum())
        fixed = max(1, used // 4)
        passed = fixed + (places - fixed + rotation * (used - fixed)) % max(1, number_of - fixed)
        return jnp.zeros((number_of,), jnp.int32).at[sequence[jnp.where(places < fixed, places, passed)]].set(jnp.asarray(tallies, jnp.int32))

    tallies = jnp.where(number % 4 == 0, named(packed, number // 4), named(usual, number - number // 4 - 1))
    mixed = jax.random.permutation(jax.random.fold_in(own, 3), number_of)
    donor, receiver = mixed[0:number_of // 2 * 2:2], mixed[1:number_of // 2 * 2:2]
    slack = jnp.minimum(tallies[donor] - 1, reach - tallies[receiver]) // 2
    slack = jnp.where((donor == sequence[0]) | (receiver == sequence[0]) | (tallies[receiver] == 0), 0, jnp.maximum(slack, 0))
    passed = jax.random.randint(jax.random.fold_in(own, 4), (number_of // 2,), 0, 1 << 20) % (slack + 1)
    tallies = tallies.at[donor].add(-passed).at[receiver].add(passed)
    labels = jnp.searchsorted(jnp.cumsum(tallies), jnp.arange(rows * top), side="right").astype(jnp.int32)
    grid = labels.reshape(top, rows).T
    grid = grid[jax.random.permutation(jax.random.fold_in(own, 1), rows)]
    rotation = jax.random.randint(jax.random.fold_in(own, 2), (rows, 1), 0, top)
    return jnp.take_along_axis(grid, (jnp.arange(top)[None, :] + rotation) % top, axis=1)


def shares(amount, total, limit, lean, full):
    weights = [(1 << 20) // math.isqrt(grade ** lean) + 1 for grade in range(1, amount + 1)]
    largest = limit if full else min(limit, max(-(-total // amount), total * weights[0] // sum(weights)))
    least = 1 if total - largest >= amount - 1 else 0
    holding, spare = [largest] + [least] * (amount - 1), total - largest - least * (amount - 1)
    while spare > 0:
        candidates = [i for i in range(1, amount) if holding[i] < largest] or [i for i in range(1, amount) if holding[i] < limit]
        whole, budget = sum([weights[i] for i in candidates]), spare
        for i in candidates:
            more = min(limit - holding[i], max(1, budget * weights[i] // whole), spare)
            holding[i] = holding[i] + more
            spare = spare - more
    return np.array(holding)


def gaussian(stream_key, dims, deviation, bound, shards=(), kind=jnp.bfloat16):
    values = deviation * jax.random.normal(stream_key, dims, jnp.float32)
    if shards:
        values = values * levels(stream_key, dims, shards, -0.22, 0.18)
    return jnp.clip(values, -bound, bound).astype(kind)


def setup_inputs(seed: int = 0, part: int = 0) -> dict:
    streams_of = jax.random.split(jax.random.key(seed), 18)
    part_keys = jax.random.split(jax.random.fold_in(streams_of[17], part), 18)
    grid_in = gaussian(part_keys[0], (GRID, C_IN), 1.0, 6.0, ((0, 16),))
    mesh_state = gaussian(streams_of[1], (MESH, D), 1.0, 6.0, ((0, 16),))
    enc_owner_keys = jax.random.split(jax.random.fold_in(streams_of[2], 1), GRID // GRID_DEV)
    enc_owner_turns = jax.random.permutation(jax.random.fold_in(streams_of[2], 3), GRID // GRID_DEV)
    enc_owner = jax.vmap(lambda own, number: shared_out(jax.random.fold_in(streams_of[2], 2), own, number, GRID_DEV, N_BAND, 1, CAP, 2))(enc_owner_keys, enc_owner_turns).reshape((GRID, 1))
    enc_slot = with_ends(jax.random.randint(streams_of[3], (GRID, 1), 0, MESH_DEV), jax.random.fold_in(streams_of[3], 1), 0, MESH_DEV - 1).astype(jnp.int32)
    dec_owner_keys = jax.random.split(jax.random.fold_in(streams_of[4], 1), GRID // GRID_DEV)
    dec_owner_turns = jax.random.permutation(jax.random.fold_in(streams_of[4], 3), GRID // GRID_DEV)
    dec_owner = jax.vmap(lambda own, number: shared_out(jax.random.fold_in(streams_of[4], 2), own, number, GRID_DEV, N_BAND, 1, CAP, 2))(dec_owner_keys, dec_owner_turns).reshape((GRID, 1))
    dec_slot = with_ends(jax.random.randint(streams_of[5], (GRID, 3), 0, MESH_DEV), jax.random.fold_in(streams_of[5], 1), 0, MESH_DEV - 1).astype(jnp.int32)
    dec_weight = jnp.clip(0.2 + 0.8 * jax.random.uniform(streams_of[6], (GRID, 3), jnp.float32) ** levels(streams_of[6], (GRID, 3), ((0, 16),), -0.2, 0.2), 0.2, 1.0)
    att_list = choose_distinct(streams_of[7], MESH_BLOCKS, 2 * BLK_DEV, NB, 0)
    w_embed = gaussian(streams_of[8], (C_IN, D), C_IN ** -0.5, 0.375)
    w_message = gaussian(streams_of[9], (D, D), D ** -0.5, 0.25)
    norm_gain = jnp.clip(1.0 + 0.18 * jax.random.normal(streams_of[10], (2 * LAYERS + 1, D), jnp.float32), 0.1, 1.9)
    w_qkv = draw_w_qkv(jax.random.fold_in(streams_of[17], 71), part)
    w_out = gaussian(streams_of[12], (LAYERS, D, D), D ** -0.5, 0.25)
    w_up = gaussian(streams_of[13], (LAYERS, D, FF), D ** -0.5, 0.25)
    w_down = gaussian(streams_of[14], (LAYERS, FF, D), FF ** -0.5, 0.125)
    w_dec1 = gaussian(streams_of[15], (D, D), D ** -0.5, 0.25)
    w_dec2 = gaussian(streams_of[16], (D, C_OUT), D ** -0.5, 0.25)
    return dict(grid_in=grid_in, mesh_state=mesh_state, enc_owner=enc_owner, enc_slot=enc_slot, dec_owner=dec_owner, dec_slot=dec_slot, dec_weight=dec_weight, att_list=att_list, w_embed=w_embed, w_message=w_message, norm_gain=norm_gain, w_qkv=w_qkv, w_out=w_out, w_up=w_up, w_down=w_down, w_dec1=w_dec1, w_dec2=w_dec2)


epsilon = 1e-05

def layer_norm(values, gains):
    average = lax.optimization_barrier(jnp.mean(values, axis=-1, keepdims=True))
    centred = values - average
    spread_sq = lax.optimization_barrier(jnp.mean(centred * centred, axis=-1, keepdims=True))
    return centred * lax.rsqrt(spread_sq + epsilon) * gains

def attention(projected, att_list):
    scaling = HD ** (-0.5)
    heads_all = projected.astype(jnp.float32).reshape(N_BAND, MESH_DEV, 3, HEADS, HD)
    highest_prec = lax.Precision.HIGHEST

    def one_shard(shard_idx):
        own_part = heads_all[shard_idx]
        earlier = heads_all[jnp.maximum(shard_idx - 1, 0)]
        later_part = heads_all[jnp.minimum(shard_idx + 1, N_BAND - 1)]
        window = jnp.concatenate([earlier, later_part], axis=0).reshape(2 * BLK_DEV, BLK, 3, HEADS, HD)
        chosen_ids = lax.dynamic_slice_in_dim(att_list, (shard_idx * BLK_DEV).astype(jnp.int32), BLK_DEV, 0).astype(jnp.int32)
        chosen = window[chosen_ids].reshape(BLK_DEV, NB * BLK, 3, HEADS, HD)
        usable = jnp.where(chosen_ids < BLK_DEV, shard_idx > 0, shard_idx < N_BAND - 1)
        usable = jnp.repeat(usable, BLK, axis=1)
        queries = own_part[:, 0]
        local_scores = jnp.einsum('qhd,khd->hqk', queries, own_part[:, 1], precision=highest_prec) * scaling
        local_scores = local_scores.reshape(HEADS, BLK_DEV, BLK, MESH_DEV)
        remote_scores = jnp.einsum('bqhd,bkhd->hbqk', queries.reshape(BLK_DEV, BLK, HEADS, HD), chosen[:, :, 1], precision=highest_prec) * scaling
        remote_scores = jnp.where(usable[None, :, None, :], remote_scores, -jnp.inf)
        highest = jnp.maximum(lax.optimization_barrier(jnp.max(local_scores, axis=-1)), lax.optimization_barrier(jnp.max(remote_scores, axis=-1)))
        local_probs = jnp.exp(local_scores - highest[..., None])
        remote_probs = jnp.exp(remote_scores - highest[..., None])
        totals = lax.optimization_barrier(jnp.sum(local_probs, axis=-1)) + lax.optimization_barrier(jnp.sum(remote_probs, axis=-1))
        local_weights = lax.optimization_barrier(local_probs.astype(jnp.bfloat16)).astype(jnp.float32)
        remote_weights = lax.optimization_barrier(remote_probs.astype(jnp.bfloat16)).astype(jnp.float32)
        combined = jnp.einsum('hbqk,khd->bqhd', local_weights, own_part[:, 2], precision=highest_prec)
        combined = combined + jnp.einsum('hbqk,bkhd->bqhd', remote_weights, chosen[:, :, 2], precision=highest_prec)
        combined = combined / jnp.transpose(totals, (1, 2, 0))[..., None]
        return combined.reshape(MESH_DEV, D).astype(jnp.bfloat16)
    return lax.map(one_shard, jnp.arange(N_BAND, dtype=jnp.int32)).reshape(MESH, D)

def reference(grid_in, mesh_state, enc_owner, enc_slot, dec_owner, dec_slot, dec_weight, att_list, w_embed, w_message, norm_gain, w_qkv, w_out, w_up, w_down, w_dec1, w_dec2):
    grid_latent = jax.nn.silu(jnp.dot(grid_in, w_embed, preferred_element_type=jnp.float32)).astype(jnp.bfloat16)
    message = jnp.dot(grid_latent, w_message, preferred_element_type=jnp.float32).astype(jnp.bfloat16)
    target = (enc_owner[:, 0] * MESH_DEV + enc_slot[:, 0]).astype(jnp.int32)
    stream = mesh_state.astype(jnp.float32) + jnp.zeros((MESH, D), jnp.float32).at[target].add(message.astype(jnp.float32))
    for layer_idx in range(LAYERS):
        normed = layer_norm(stream, norm_gain[2 * layer_idx]).astype(jnp.bfloat16)
        projected = jnp.dot(normed, w_qkv[layer_idx], preferred_element_type=jnp.float32).astype(jnp.bfloat16)
        attended = attention(projected, att_list)
        stream = stream + jnp.dot(attended, w_out[layer_idx], preferred_element_type=jnp.float32)
        normed = layer_norm(stream, norm_gain[2 * layer_idx + 1]).astype(jnp.bfloat16)
        hidden = jax.nn.silu(jnp.dot(normed, w_up[layer_idx], preferred_element_type=jnp.float32)).astype(jnp.bfloat16)
        stream = stream + jnp.dot(hidden, w_down[layer_idx], preferred_element_type=jnp.float32)
    final = layer_norm(stream, norm_gain[2 * LAYERS]).astype(jnp.bfloat16)

    def decode(block_idx):
        offset = (block_idx * GRID_DEV).astype(jnp.int32)
        latent_rows = lax.dynamic_slice_in_dim(grid_latent, offset, GRID_DEV, 0)
        owners = lax.dynamic_slice_in_dim(dec_owner, offset, GRID_DEV, 0)
        slot_ids = lax.dynamic_slice_in_dim(dec_slot, offset, GRID_DEV, 0)
        weights = lax.dynamic_slice_in_dim(dec_weight, offset, GRID_DEV, 0)
        node_ids = (owners * MESH_DEV + slot_ids).astype(jnp.int32)
        row_data = final[node_ids].astype(jnp.float32)
        pulled = lax.optimization_barrier(jnp.sum(weights[:, :, None] * row_data, axis=1))
        pulled = lax.optimization_barrier(pulled.astype(jnp.bfloat16)).astype(jnp.float32)
        mixed = (latent_rows.astype(jnp.float32) + pulled).astype(jnp.bfloat16)
        decoded = jax.nn.silu(jnp.dot(mixed, w_dec1, preferred_element_type=jnp.float32)).astype(jnp.bfloat16)
        return jnp.dot(decoded, w_dec2, preferred_element_type=jnp.float32).astype(jnp.bfloat16)
    result = lax.map(decode, jnp.arange(N_BAND, dtype=jnp.int32)).reshape(GRID, C_OUT)
    return jnp.transpose(result)
```

```python
import functools

import jax
import jax.numpy as jnp
from jax import lax
from jax.experimental import pallas as pl
from jax.experimental.pallas import tpu as pltpu
from jax.sharding import PartitionSpec as P

HEADS = 4
BLK = 128
NB = 4
META = 16
ROWS = 512
RET = 96
LOW = 32
MASKED = -1e30
VMEM_LIMIT = 40 * 1024 * 1024

epsilon = 1e-05

F32 = jnp.float32
BF16 = jnp.bfloat16


def dot(a, b):
    return jnp.dot(a, b, preferred_element_type=F32)


def dot_nt(a, b):
    return lax.dot_general(a, b, (((1,), (1,)), ((), ())), preferred_element_type=F32)


def silu(v):
    return v / (1.0 + jnp.exp(-v))


def layer_norm(values, gains):
    average = jnp.mean(values, axis=-1, keepdims=True)
    centred = values - average
    spread_sq = jnp.mean(centred * centred, axis=-1, keepdims=True)
    return centred * lax.rsqrt(spread_sq + epsilon) * gains


def call(kernel, out_shape, args, scratch=(), smem=(), flops=0, moved=0):
    specs = [
        pl.BlockSpec(memory_space=pltpu.SMEM if i in smem else pltpu.VMEM)
        for i in range(len(args))
    ]
    outs = jax.tree.map(lambda _: pl.BlockSpec(memory_space=pltpu.VMEM), out_shape)
    return pl.pallas_call(
        kernel,
        out_shape=out_shape,
        in_specs=specs,
        out_specs=outs,
        scratch_shapes=list(scratch),
        compiler_params=pltpu.CompilerParams(vmem_limit_bytes=VMEM_LIMIT),
        cost_estimate=pl.CostEstimate(flops=flops, bytes_accessed=moved, transcendentals=0),
    )(*args)


def owner_onehot(owner, peers):
    places = lax.broadcasted_iota(jnp.int32, (peers, owner.shape[1]), 0)
    return jnp.where(places == owner, 1.0, 0.0).astype(F32)


def rank_onehot(rank, cap):
    places = lax.broadcasted_iota(jnp.int32, (cap, rank.shape[1]), 0).astype(F32)
    return jnp.where(places == rank, 1.0, 0.0).astype(BF16)


def bucket_kernel(peers, cap, weighted, *refs):
    if weighted:
        owner_ref, slot_ref, weight_ref, rows_ref, out_ref, rank_ref = refs
    else:
        owner_ref, slot_ref, rows_ref, out_ref, rank_ref = refs
    grid, width = rows_ref.shape
    part = 256 if grid % 256 == 0 else grid
    chosen = owner_onehot(owner_ref[...], peers)
    chosen16 = chosen.astype(BF16)
    upto = jnp.where(
        lax.broadcasted_iota(jnp.int32, (part, part), 0)
        <= lax.broadcasted_iota(jnp.int32, (part, part), 1),
        1.0,
        0.0,
    ).astype(BF16)
    carry = jnp.zeros((peers, 1), F32)
    ranks = []
    for c in range(grid // part):
        span = slice(c * part, (c + 1) * part)
        counts = dot(chosen16[:, span], upto) + carry
        carry = counts[:, part - 1 :]
        ranks.append(jnp.sum(chosen[:, span] * counts, axis=0, keepdims=True) - 1.0)
    rank = jnp.concatenate(ranks, axis=1)
    rank_ref[...] = rank
    placed = rank_onehot(rank, cap)

    slots = slot_ref[...]
    pieces = [(slots // LOW).astype(F32), (slots % LOW).astype(F32)]
    if weighted:
        weights = weight_ref[...]
        upper = weights.astype(BF16).astype(F32)
        pieces += [upper, weights - upper]
    held = sum(p.shape[0] for p in pieces)
    pieces.append(jnp.zeros((META - held, grid), F32))
    features = jnp.concatenate(pieces, axis=0).astype(BF16).astype(F32)
    spread = (chosen[:, None, :] * features[None, :, :]).reshape(peers * META, grid)
    meta = dot_nt(spread.astype(BF16), placed).reshape(peers, META, cap)
    out_ref[:, cap:, :] = jnp.zeros((peers, META, width), BF16)
    out_ref[:, cap:, :cap] = meta.astype(BF16)

    rows = rows_ref[...]
    step = ROWS // cap
    for o in range(0, peers, step):
        select = (chosen16[o : o + step, None, :] * placed[None, :, :]).reshape(step * cap, grid)
        moved = dot(select, rows)
        out_ref[o : o + step, :cap, :] = moved.astype(BF16).reshape(step, cap, width)


def bucket(owner, slots, weights, rows, peers, cap):
    grid, width = rows.shape
    weighted = weights is not None
    args = (owner, slots) + ((weights,) if weighted else ()) + (rows,)
    return call(
        functools.partial(bucket_kernel, peers, cap, weighted),
        (
            jax.ShapeDtypeStruct((peers, cap + META, width), BF16),
            jax.ShapeDtypeStruct((1, grid), F32),
        ),
        args,
        flops=2 * peers * cap * grid * width,
        moved=2 * (grid * width + peers * (cap + META) * width),
    )


def slot_row(got_ref, o, step, cap, low, count):
    def piece(r):
        rows = got_ref[r, cap:, :cap].astype(F32)
        upper = rows[low : low + 1, :]
        lower = rows[low + count : low + count + 1, :]
        return upper * LOW + lower

    return jnp.concatenate([piece(r) for r in range(o, o + step)], axis=1)


def weight_row(got_ref, o, step, cap, first):
    def piece(r):
        rows = got_ref[r, cap:, :cap].astype(F32)
        return rows[first : first + 1, :] + rows[first + 3 : first + 4, :]

    return jnp.concatenate([piece(r) for r in range(o, o + step)], axis=1)


def encode_kernel(peers, cap, got_ref, state_ref, embed_ref, message_ref, gain_ref, stream_ref, normed_ref):
    width = got_ref.shape[2]
    nodes = state_ref.shape[0]
    step = ROWS // cap
    stream_ref[...] = state_ref[...].astype(F32)
    for o in range(0, peers, step):
        rows = got_ref[o : o + step, :cap, :].reshape(ROWS, width)
        latent = silu(dot(rows, embed_ref[...])).astype(BF16)
        message = dot(latent, message_ref[...]).astype(BF16)
        slot = slot_row(got_ref, o, step, cap, 0, 1)
        places = lax.broadcasted_iota(jnp.int32, (nodes, ROWS), 0).astype(F32)
        target = jnp.where(places == slot, 1.0, 0.0).astype(BF16)
        stream_ref[...] += dot(target, message)
    normed_ref[...] = layer_norm(stream_ref[...], gain_ref[0:1, :]).astype(BF16)


def local_kernel(normed_ref, qkv_ref, query_ref, partial_ref, stats_ref):
    nodes, width = normed_ref.shape
    head = width // HEADS
    scaling = head ** (-0.5)
    normed = normed_ref[...]
    query = dot(normed, qkv_ref[:, :width]).astype(BF16)
    key = dot(normed, qkv_ref[:, width : 2 * width]).astype(BF16)
    value = dot(normed, qkv_ref[:, 2 * width :]).astype(BF16)
    query_ref[...] = query
    stats = []
    for h in range(HEADS):
        cols = slice(h * head, (h + 1) * head)
        scores = dot_nt(query[:, cols], key[:, cols]) * scaling
        highest = jnp.max(scores, axis=-1, keepdims=True)
        probs = jnp.exp(scores - highest)
        stats += [highest, jnp.sum(probs, axis=-1, keepdims=True)]
        partial_ref[:, cols] = dot(probs.astype(BF16), value[:, cols])
    lanes = lax.broadcasted_iota(jnp.int32, (nodes, BLK), 1)
    packed = jnp.zeros((nodes, BLK), F32)
    for i, s in enumerate(stats):
        packed = jnp.where(lanes == i, s, packed)
    stats_ref[...] = packed


def mesh_kernel(
    where_ref,
    att_ref,
    before_ref,
    after_ref,
    query_ref,
    partial_ref,
    stats_ref,
    stream_ref,
    qkv_ref,
    out_w_ref,
    up_ref,
    down_ref,
    gain_ref,
    final_ref,
    side_ref,
    attended_ref,
):
    nodes, width = stream_ref.shape
    head = width // HEADS
    blocks = nodes // BLK
    scaling = head ** (-0.5)
    has_before = where_ref[0] > 0
    has_after = where_ref[0] < where_ref[1] - 1
    kv = qkv_ref[:, width:]
    side_ref[:nodes, :] = dot(before_ref[...], kv).astype(BF16)
    side_ref[nodes:, :] = dot(after_ref[...], kv).astype(BF16)
    for i in range(blocks):
        rows = slice(i * BLK, (i + 1) * BLK)
        starts = [pl.multiple_of(att_ref[i, k] * BLK, BLK) for k in range(NB)]
        usable = [
            jnp.where(att_ref[i, k] < blocks, has_before, has_after) for k in range(NB)
        ]
        chosen = jnp.concatenate([side_ref[pl.ds(s, BLK), :] for s in starts], axis=0)
        allowed = jnp.concatenate(
            [jnp.full((1, BLK), jnp.where(u, 1.0, 0.0), F32) for u in usable], axis=1
        )
        for h in range(HEADS):
            cols = slice(h * head, (h + 1) * head)
            vcols = slice(width + h * head, width + (h + 1) * head)
            scores = dot_nt(query_ref[rows, cols], chosen[:, cols]) * scaling
            scores = jnp.where(allowed > 0.5, scores, MASKED)
            held = stats_ref[rows, 2 * h : 2 * h + 1]
            highest = jnp.maximum(held, jnp.max(scores, axis=-1, keepdims=True))
            probs = jnp.exp(scores - highest)
            keep = jnp.exp(held - highest)
            totals = stats_ref[rows, 2 * h + 1 : 2 * h + 2] * keep + jnp.sum(
                probs, axis=-1, keepdims=True
            )
            combined = partial_ref[rows, cols] * keep + dot(probs.astype(BF16), chosen[:, vcols])
            attended_ref[rows, cols] = (combined / totals).astype(BF16)
    stream = stream_ref[...] + dot(attended_ref[...], out_w_ref[...])
    normed = layer_norm(stream, gain_ref[1:2, :]).astype(BF16)
    hidden_width = up_ref.shape[1]
    for c in range(0, hidden_width, width):
        hidden = silu(dot(normed, up_ref[:, c : c + width])).astype(BF16)
        stream = stream + dot(hidden, down_ref[c : c + width, :])
    final = layer_norm(stream, gain_ref[2:3, :])
    final_ref[...] = final.T.astype(BF16)


def decode_kernel(peers, cap, got_ref, final_ref, embed_ref, dec1_ref, dec2_ref, out_ref):
    width = got_ref.shape[2]
    nodes = final_ref.shape[1]
    channels = dec2_ref.shape[0]
    step = ROWS // cap
    final = final_ref[...]
    for o in range(0, peers, step):
        rows = got_ref[o : o + step, :cap, :].reshape(ROWS, width)
        latent = silu(dot_nt(embed_ref[...], rows)).astype(BF16)
        places = lax.broadcasted_iota(jnp.int32, (nodes, ROWS), 0).astype(F32)
        mix = jnp.zeros((nodes, ROWS), F32)
        for k in range(3):
            slot = slot_row(got_ref, o, step, cap, k, 3)
            weight = weight_row(got_ref, o, step, cap, 6 + k)
            mix = mix + jnp.where(places == slot, weight, 0.0)
        upper = mix.astype(BF16)
        lower = (mix - upper.astype(F32)).astype(BF16)
        pulled = (dot(final, upper) + dot(final, lower)).astype(BF16)
        mixed = (latent.astype(F32) + pulled.astype(F32)).astype(BF16)
        decoded = silu(dot(dec1_ref[...], mixed)).astype(BF16)
        result = dot(dec2_ref[...], decoded).astype(BF16)
        for r in range(step):
            out_ref[o + r, :channels, :] = result[:, r * cap : (r + 1) * cap]
            out_ref[o + r, channels:, :] = jnp.zeros((RET - channels, cap), BF16)


def return_kernel(peers, cap, got_ref, owner_ref, rank_ref, out_ref):
    channels, grid = out_ref.shape
    placed = rank_onehot(rank_ref[...], cap)
    chosen = owner_onehot(owner_ref[...], peers)
    total = jnp.zeros((RET, grid), F32)
    step = 4
    for o in range(0, peers, step):
        spread = dot(got_ref[o : o + step].reshape(step * RET, cap), placed)
        for r in range(step):
            total = total + spread[r * RET : (r + 1) * RET] * chosen[o + r : o + r + 1, :]
    out_ref[...] = total[:channels].astype(BF16)


def body(
    grid_in,
    mesh_state,
    enc_owner,
    enc_slot,
    dec_owner,
    dec_slot,
    dec_weight,
    att_list,
    w_embed,
    w_message,
    norm_gain,
    w_qkv,
    w_out,
    w_up,
    w_down,
    w_dec1,
    w_dec2,
):
    peers = lax.axis_size("band")
    place = lax.axis_index("band")
    grid = grid_in.shape[0]
    nodes, width = mesh_state.shape
    cap = 2 * grid // peers
    channels = w_dec2.shape[1]
    slots = peers * cap

    def exchange(x):
        return lax.all_to_all(x, "band", split_axis=0, concat_axis=0, tiled=True)

    enc_send, _ = bucket(enc_owner.T, enc_slot.T, None, grid_in, peers, cap)
    enc_got = exchange(enc_send)
    dec_send, dec_rank = bucket(dec_owner.T, dec_slot.T, dec_weight.T, grid_in, peers, cap)
    dec_got = exchange(dec_send)

    stream, normed = call(
        functools.partial(encode_kernel, peers, cap),
        (
            jax.ShapeDtypeStruct((nodes, width), F32),
            jax.ShapeDtypeStruct((nodes, width), BF16),
        ),
        (enc_got, mesh_state, w_embed, w_message, norm_gain),
        flops=2 * slots * width * (grid_in.shape[1] + width + nodes),
        moved=2 * slots * grid_in.shape[1] + 8 * nodes * width,
    )
    up = [(i, i + 1) for i in range(peers - 1)]
    down = [(j, i) for i, j in up]
    before = lax.ppermute(normed, "band", up)
    after = lax.ppermute(normed, "band", down)
    query, partial, stats = call(
        local_kernel,
        (
            jax.ShapeDtypeStruct((nodes, width), BF16),
            jax.ShapeDtypeStruct((nodes, width), F32),
            jax.ShapeDtypeStruct((nodes, BLK), F32),
        ),
        (normed, w_qkv[0]),
        flops=2 * nodes * width * (3 * width + 2 * nodes),
        moved=2 * nodes * width * 8,
    )
    where = jnp.stack([place, jnp.int32(peers)]).astype(jnp.int32)
    final = call(
        mesh_kernel,
        jax.ShapeDtypeStruct((width, nodes), BF16),
        (
            where,
            att_list,
            before,
            after,
            query,
            partial,
            stats,
            stream,
            w_qkv[0],
            w_out[0],
            w_up[0],
            w_down[0],
            norm_gain,
        ),
        scratch=(
            pltpu.VMEM((2 * nodes, 2 * width), BF16),
            pltpu.VMEM((nodes, width), BF16),
        ),
        smem=(0, 1),
        flops=2 * nodes * width * (4 * width + 2 * nodes + width + 2 * w_up.shape[2]),
        moved=2 * width * (3 * width + width + 2 * w_up.shape[2]) + 10 * nodes * width,
    )
    result = call(
        functools.partial(decode_kernel, peers, cap),
        jax.ShapeDtypeStruct((peers, RET, cap), BF16),
        (dec_got, final, w_embed.T, w_dec1.T, w_dec2.T),
        flops=2 * slots * width * (grid_in.shape[1] + 2 * nodes + width + 128),
        moved=2 * slots * grid_in.shape[1] + 2 * nodes * width,
    )
    returned = exchange(result)
    return call(
        functools.partial(return_kernel, peers, cap),
        jax.ShapeDtypeStruct((channels, grid), BF16),
        (returned, dec_owner.T, dec_rank),
        flops=2 * peers * RET * cap * grid,
        moved=2 * slots * RET,
    )


def solution(mesh):
    return jax.shard_map(
        body,
        mesh=mesh,
        in_specs=(
            P(("ens", "band"), None),
            P("band", None),
            P("band", None),
            P("band", None),
            P("band", None),
            P("band", None),
            P("band", None),
            P("band", None),
            P(),
            P(),
            P(),
            P(),
            P(),
            P(),
            P(),
            P(),
            P(),
        ),
        out_specs=P(None, ("ens", "band")),
        check_vma=False,
    )
```

```python
import functools

import jax
import jax.numpy as jnp
from jax import lax
from jax.experimental import pallas as pl
from jax.experimental.pallas import tpu as pltpu
from jax.sharding import PartitionSpec as P

HEADS = 4
BLK = 128
NB = 4
META = 16
ROWS = 512
LOW = 32
MASKED = -1e30
LOG2E = 1.4426950408889634
VMEM_LIMIT = 24 * 1024 * 1024

epsilon = 1e-05

F32 = jnp.float32
BF16 = jnp.bfloat16


def dot(a, b):
    return jnp.dot(a, b, preferred_element_type=F32)


def dot_nt(a, b):
    return lax.dot_general(a, b, (((1,), (1,)), ((), ())), preferred_element_type=F32)


def silu(v):
    half = 0.5 * v
    return half + half * jnp.tanh(half)


def layer_norm(values, gains):
    average = jnp.mean(values, axis=-1, keepdims=True)
    centred = values - average
    spread_sq = jnp.mean(centred * centred, axis=-1, keepdims=True)
    return centred * lax.rsqrt(spread_sq + epsilon) * gains


class Held:
    def __init__(self, far, near, sem):
        self.near = near
        self.copy = pltpu.make_async_copy(far, near, sem)
        self.state = 0

    def start(self):
        if self.state == 0:
            self.copy.start()
            self.state = 1

    def __call__(self):
        self.start()
        if self.state == 1:
            self.copy.wait()
            self.state = 2
        return self.near


class Sent:
    def __init__(self, near, far, sem):
        self.near = near
        self.copy = pltpu.make_async_copy(near, far, sem)
        self.started = False

    def send(self):
        if not self.started:
            self.copy.start()
            self.started = True


def call(kernel, outs, args, kinds, scratch=(), late=(), flops=0, moved=0):
    n_in, n_out = len(args), len(outs)
    far_in = [i for i in range(n_in) if kinds[i] == "H"]
    far_out = [i for i in range(n_out) if outs[i][2] == "H"]

    def wrapped(*refs):
        ins, results = list(refs[:n_in]), list(refs[n_in : n_in + n_out])
        rest = list(refs[n_in + n_out :])
        sems = rest.pop(0)
        for n, i in enumerate(far_in):
            ins[i] = Held(ins[i], rest.pop(0), sems.at[n])
            if i not in late:
                ins[i].start()
        for n, i in enumerate(far_out):
            results[i] = Sent(rest.pop(0), results[i], sems.at[len(far_in) + n])
        kernel(*ins, *results, *rest)
        for i in far_out:
            results[i].send()
        for i in far_in:
            ins[i]()
        for i in far_out:
            results[i].copy.wait()

    spaces = {"V": pltpu.VMEM, "H": pltpu.HBM, "S": pltpu.SMEM}

    def spec(kind):
        return pl.BlockSpec(memory_space=pl.ANY if kind == "H" else spaces[kind])

    def placed(x, kind):
        return x if kind == "S" else pltpu.with_memory_space_constraint(x, spaces[kind])

    return pl.pallas_call(
        wrapped,
        out_shape=tuple(
            pltpu.HBM(shape, dtype) if kind == "H" else jax.ShapeDtypeStruct(shape, dtype)
            for shape, dtype, kind in outs
        ),
        in_specs=[spec(kind) for kind in kinds],
        out_specs=tuple(spec(kind) for _, _, kind in outs),
        scratch_shapes=[pltpu.SemaphoreType.DMA((max(1, len(far_in) + len(far_out)),))]
        + [pltpu.VMEM(args[i].shape, args[i].dtype) for i in far_in]
        + [pltpu.VMEM(outs[i][0], outs[i][1]) for i in far_out]
        + list(scratch),
        compiler_params=pltpu.CompilerParams(vmem_limit_bytes=VMEM_LIMIT),
        cost_estimate=pl.CostEstimate(flops=flops, bytes_accessed=moved, transcendentals=0),
    )(*[placed(x, kind) for x, kind in zip(args, kinds)])


def owner_onehot(owner, peers):
    places = lax.broadcasted_iota(jnp.int32, (peers, owner.shape[1]), 0)
    return jnp.where(places == owner, 1.0, 0.0).astype(F32)


def rank_onehot(rank, cap):
    places = lax.broadcasted_iota(jnp.int32, (cap, rank.shape[1]), 0).astype(F32)
    return jnp.where(places == rank, 1.0, 0.0).astype(BF16)


def bucket_kernel(peers, cap, weighted, turned, *refs):
    refs = list(refs)
    held_owner, held_slot = refs.pop(0), refs.pop(0)
    held_weight = refs.pop(0) if weighted else None
    held_rows = refs.pop(0)
    turns = [refs.pop(0) for _ in range(turned)]
    out, rank_out = refs.pop(0), refs.pop(0) if weighted else None
    turned_outs = [refs.pop(0) for _ in range(turned)]
    send_ref = out.near
    grid, width = held_rows.near.shape
    part = 256 if grid % 256 == 0 else grid
    upto = jnp.where(
        lax.broadcasted_iota(jnp.int32, (part, part), 0)
        <= lax.broadcasted_iota(jnp.int32, (part, part), 1),
        1.0,
        0.0,
    ).astype(BF16)
    owner = held_owner()[...]
    chosen = owner_onehot(owner, peers)
    chosen16 = chosen.astype(BF16)
    carry = jnp.zeros((peers, 1), F32)
    ranks = []
    for c in range(grid // part):
        span = slice(c * part, (c + 1) * part)
        counts = dot(chosen16[:, span], upto) + carry
        carry = counts[:, part - 1 :]
        ranks.append(jnp.sum(chosen[:, span] * counts, axis=0, keepdims=True) - 1.0)
    rank = jnp.concatenate(ranks, axis=1)
    if weighted:
        rank_out.near[...] = rank
    placed = rank_onehot(rank, cap)

    slots = held_slot()[...]
    pieces = [(slots // LOW).astype(F32), (slots % LOW).astype(F32)]
    if weighted:
        pieces.append(held_weight()[...])
    used = sum(p.shape[0] for p in pieces)
    pieces.append(jnp.zeros((META - used, grid), F32))
    features = jnp.concatenate(pieces, axis=0).astype(BF16).astype(F32)
    spread = (chosen[:, None, :] * features[None, :, :]).reshape(peers * META, grid)
    meta = dot_nt(spread.astype(BF16), placed).reshape(peers, META, cap)
    send_ref[:, cap:, :] = jnp.zeros((peers, META, width), BF16)
    send_ref[:, cap:, :cap] = meta.astype(BF16)

    rows = held_rows()[...]
    step = ROWS // cap
    for o in range(0, peers, step):
        select = (chosen16[o : o + step, None, :] * placed[None, :, :]).reshape(step * cap, grid)
        moved = dot(select, rows)
        send_ref[o : o + step, :cap, :] = moved.astype(BF16).reshape(step, cap, width)
    out.send()
    for f, t in zip(turns, turned_outs):
        t.near[...] = f()[...].T


def bucket(owner, slots, weights, rows, turns, peers, cap):
    grid, width = rows.shape
    weighted = weights is not None
    args = (owner, slots) + ((weights,) if weighted else ()) + (rows,) + turns
    outs = [((peers, cap + META, width), BF16, "H")]
    if weighted:
        outs.append(((1, grid), F32, "H"))
    outs += [(x.shape[::-1], x.dtype, "H") for x in turns]
    return call(
        functools.partial(bucket_kernel, peers, cap, weighted, len(turns)),
        outs,
        args,
        "H" * len(args),
        flops=2 * peers * cap * grid * width,
        moved=2 * (grid * width + peers * (cap + META) * width),
    )


def meta_row(got_ref, o, step, cap, row):
    return jnp.concatenate(
        [got_ref[r, cap:, :cap].astype(F32)[row : row + 1, :] for r in range(o, o + step)],
        axis=1,
    )


def slot_row(got_ref, o, step, cap, low, count):
    return meta_row(got_ref, o, step, cap, low) * LOW + meta_row(
        got_ref, o, step, cap, low + count
    )


def encode_kernel(peers, cap, got_ref, embed, message_w, state, gain, stream, normed, target_ref):
    width = got_ref.shape[2]
    nodes = stream.near.shape[0]
    step = ROWS // cap
    places = lax.broadcasted_iota(jnp.int32, (nodes, ROWS), 0).astype(F32)
    for n, o in enumerate(range(0, peers, step)):
        slot = slot_row(got_ref, o, step, cap, 0, 1)
        target_ref[n] = jnp.where(places == slot, 1.0, 0.0).astype(BF16)
    total = None
    for n, o in enumerate(range(0, peers, step)):
        rows = got_ref[o : o + step, :cap, :].reshape(ROWS, width)
        latent = silu(dot(rows, embed()[...])).astype(BF16)
        message = dot(latent, message_w()[...]).astype(BF16)
        arrived = dot(target_ref[n], message)
        total = state()[...].astype(F32) + arrived if total is None else total + arrived
    normed.near[...] = layer_norm(total, gain()[0:1, :]).astype(BF16)
    normed.send()
    stream.near[...] = total


def local_kernel(normed, qkv, query, partial, stats):
    nodes, width = query.near.shape
    head = width // HEADS
    rate = head ** (-0.5) * LOG2E
    held = normed()[...]
    qkv_ref = qkv()
    queries = dot(held, qkv_ref[:, :width]).astype(BF16)
    query.near[...] = queries
    query.send()
    key = dot(held, qkv_ref[:, width : 2 * width]).astype(BF16)
    value = dot(held, qkv_ref[:, 2 * width :]).astype(BF16)
    ones = jnp.ones((nodes, BLK), BF16)
    lanes = lax.broadcasted_iota(jnp.int32, (nodes, BLK), 1)
    packed = jnp.zeros((nodes, BLK), F32)
    for h in range(HEADS):
        cols = slice(h * head, (h + 1) * head)
        scores = dot_nt(queries[:, cols], key[:, cols])
        highest = jnp.max(scores, axis=-1, keepdims=True)
        weights = jnp.exp2((scores - highest) * rate).astype(BF16)
        sums = dot(weights, jnp.concatenate([value[:, cols], ones], axis=1))
        partial.near[:, cols] = sums[:, :head]
        packed = jnp.where(lanes == h, highest, packed)
        packed = jnp.where(lanes == HEADS + h, sums[:, head:], packed)
    stats.near[...] = packed


def tail_kernel(
    peers,
    cap,
    where_ref,
    att_ref,
    before_ref,
    after_ref,
    got_ref,
    qkv,
    query,
    stats,
    partial,
    stream_in,
    out_w,
    up_w,
    down_w,
    gain,
    embed,
    dec1,
    dec2,
    out_ref,
    key_ref,
    value_ref,
    attended_ref,
    mix_ref,
):
    nodes, width = attended_ref.shape
    head = width // HEADS
    blocks = nodes // BLK
    rate = head ** (-0.5) * LOG2E
    has_before = where_ref[0] > 0
    has_after = where_ref[0] < where_ref[1] - 1
    step = ROWS // cap
    columns = got_ref.shape[2]

    places = lax.broadcasted_iota(jnp.int32, (nodes, ROWS), 0).astype(F32)
    for n, o in enumerate(range(0, peers, step)):
        mix = jnp.zeros((nodes, ROWS), F32)
        for k in range(3):
            slot = slot_row(got_ref, o, step, cap, k, 3)
            weight = meta_row(got_ref, o, step, cap, 6 + k)
            mix = mix + jnp.where(places == slot, weight, 0.0)
        mix_ref[n] = mix.astype(BF16)

    qkv_ref = qkv()
    for n, side in enumerate((before_ref, after_ref)):
        rows = slice(n * nodes, (n + 1) * nodes)
        key_ref[rows, :] = dot(side[...], qkv_ref[:, width : 2 * width]).astype(BF16)
        value = dot(side[...], qkv_ref[:, 2 * width :]).astype(BF16)
        for h in range(HEADS):
            value_ref[rows, 2 * h * head : (2 * h + 1) * head] = value[:, h * head : (h + 1) * head]
    for h in range(HEADS):
        value_ref[:, (2 * h + 1) * head : (2 * h + 2) * head] = jnp.ones((2 * nodes, head), BF16)

    query_ref, stats_ref, partial_ref = query(), stats(), partial()
    starts, allowed = [], []
    for i in range(blocks):
        starts.append([pl.multiple_of(att_ref[i, k] * BLK, BLK) for k in range(NB)])
        usable = [
            jnp.where(att_ref[i, k] < blocks, has_before, has_after) for k in range(NB)
        ]
        row = jnp.concatenate(
            [jnp.full((1, BLK), jnp.where(u, 0.0, MASKED), F32) for u in usable], axis=1
        )
        allowed.append(row)

    def chosen(ref, i, span):
        return jnp.concatenate([ref[pl.ds(s, BLK), span] for s in starts[i]], axis=0)

    for h in range(HEADS):
        cols = slice(h * head, (h + 1) * head)
        both = slice(2 * h * head, (2 * h + 2) * head)
        scores = jnp.concatenate(
            [
                dot_nt(query_ref[i * BLK : (i + 1) * BLK, cols], chosen(key_ref, i, cols))
                + allowed[i]
                for i in range(blocks)
            ],
            axis=0,
        )
        held = stats_ref[:, h : h + 1]
        highest = jnp.maximum(held, jnp.max(scores, axis=-1, keepdims=True))
        weights = jnp.exp2((scores - highest) * rate).astype(BF16)
        keep = jnp.exp2((held - highest) * rate)
        sums = jnp.concatenate(
            [
                dot(weights[i * BLK : (i + 1) * BLK], chosen(value_ref, i, both))
                for i in range(blocks)
            ],
            axis=0,
        )
        totals = stats_ref[:, HEADS + h : HEADS + h + 1] * keep + sums[:, head:]
        combined = partial_ref[:, cols] * keep + sums[:, :head]
        attended_ref[:, cols] = (combined / totals).astype(BF16)

    stream = stream_in()[...] + dot(attended_ref[...], out_w()[...])
    normed = layer_norm(stream, gain()[1:2, :]).astype(BF16)
    up_ref, down_ref = up_w(), down_w()
    hidden_width = up_ref.shape[1]
    for c in range(0, hidden_width, width):
        hidden = silu(dot(normed, up_ref[:, c : c + width])).astype(BF16)
        stream = stream + dot(hidden, down_ref[c : c + width, :])
    final = layer_norm(stream, gain()[2:3, :]).astype(BF16).T

    embed_ref, dec1_ref, dec2_ref = embed(), dec1(), dec2()
    for n, o in enumerate(range(0, peers, step)):
        rows = got_ref[o : o + step, :cap, :].reshape(ROWS, columns)
        latent = silu(dot_nt(embed_ref[...], rows)).astype(BF16)
        pulled = dot(final, mix_ref[n]).astype(BF16)
        mixed = (latent.astype(F32) + pulled.astype(F32)).astype(BF16)
        decoded = silu(dot(dec1_ref[...], mixed)).astype(BF16)
        result = dot(dec2_ref[...], decoded).astype(BF16)
        for r in range(step):
            out_ref[o + r] = result[:, r * cap : (r + 1) * cap]


TAIL_KINDS = "SSVVVHHHHHHHHHHHH"


def tail_scratch(nodes, width, slots):
    return (
        pltpu.VMEM((2 * nodes, width), BF16),
        pltpu.VMEM((2 * nodes, 2 * width), BF16),
        pltpu.VMEM((nodes, width), BF16),
        pltpu.VMEM((slots // ROWS, nodes, ROWS), BF16),
    )


def return_kernel(peers, cap, got_ref, rank, owner, out_ref):
    channels, grid = out_ref.shape
    placed = rank_onehot(rank[...], cap)
    chosen = owner_onehot(owner[...], peers)
    total = jnp.zeros((channels, grid), F32)
    for o in range(peers):
        total = total + dot(got_ref[o], placed) * chosen[o : o + 1, :]
    out_ref[...] = total.astype(BF16)


def body(
    grid_in,
    mesh_state,
    enc_owner,
    enc_slot,
    dec_owner,
    dec_slot,
    dec_weight,
    att_list,
    w_embed,
    w_message,
    norm_gain,
    w_qkv,
    w_out,
    w_up,
    w_down,
    w_dec1,
    w_dec2,
):
    peers = lax.axis_size("band")
    place = lax.axis_index("band")
    grid = grid_in.shape[0]
    nodes, width = mesh_state.shape
    cap = 2 * grid // peers
    channels = w_dec2.shape[1]
    slots = peers * cap

    def exchange(x):
        return lax.all_to_all(x, "band", split_axis=0, concat_axis=0, tiled=True)

    (enc_send,) = bucket(enc_owner.T, enc_slot.T, None, grid_in, (), peers, cap)
    enc_got = exchange(enc_send)
    dec_send, rank, embed_t, dec1_t = bucket(
        dec_owner.T, dec_slot.T, dec_weight.T, grid_in, (w_embed, w_dec1), peers, cap
    )
    dec_got = exchange(dec_send)

    stream, normed = call(
        functools.partial(encode_kernel, peers, cap),
        (((nodes, width), F32, "H"), ((nodes, width), BF16, "H")),
        (enc_got, w_embed, w_message, mesh_state, norm_gain),
        "VHHHH",
        scratch=(pltpu.VMEM((slots // ROWS, nodes, ROWS), BF16),),
        flops=2 * slots * width * (grid_in.shape[1] + width + nodes),
        moved=2 * slots * grid_in.shape[1] + 8 * nodes * width,
    )
    up = [(i, i + 1) for i in range(peers - 1)]
    down = [(j, i) for i, j in up]
    before = lax.ppermute(normed, "band", up)
    after = lax.ppermute(normed, "band", down)
    query, partial, stats = call(
        local_kernel,
        (((nodes, width), BF16, "H"), ((nodes, width), F32, "H"), ((nodes, BLK), F32, "H")),
        (normed, w_qkv[0]),
        "HH",
        flops=2 * nodes * width * (3 * width + 2 * nodes),
        moved=2 * nodes * width * 8,
    )
    where = jnp.stack([place, jnp.int32(peers)]).astype(jnp.int32)
    (result,) = call(
        functools.partial(tail_kernel, peers, cap),
        (((peers, channels, cap), BF16, "V"),),
        (
            where,
            att_list,
            before,
            after,
            dec_got,
            w_qkv[0],
            query,
            stats,
            partial,
            stream,
            w_out[0],
            w_up[0],
            w_down[0],
            norm_gain,
            embed_t,
            dec1_t,
            w_dec2.T,
        ),
        TAIL_KINDS,
        scratch=tail_scratch(nodes, width, slots),
        flops=2 * nodes * width * (4 * width + 2 * nodes + width + 2 * w_up.shape[2])
        + 2 * slots * width * (grid_in.shape[1] + nodes + width + 128),
        moved=2 * width * (3 * width + width + 2 * w_up.shape[2]) + 10 * nodes * width,
    )
    returned = exchange(result)
    (denoised,) = call(
        functools.partial(return_kernel, peers, cap),
        (((channels, grid), BF16, "V"),),
        (returned, rank, dec_owner.T),
        "VVV",
        flops=2 * slots * channels * grid,
        moved=2 * slots * channels,
    )
    return denoised


def solution(mesh):
    return jax.shard_map(
        body,
        mesh=mesh,
        in_specs=(
            P(("ens", "band"), None),
            P("band", None),
            P("band", None),
            P("band", None),
            P("band", None),
            P("band", None),
            P("band", None),
            P("band", None),
            P(),
            P(),
            P(),
            P(),
            P(),
            P(),
            P(),
            P(),
            P(),
        ),
        out_specs=P(None, ("ens", "band")),
        check_vma=False,
    )
```

```python
import functools

import jax
import jax.numpy as jnp
from jax import lax
from jax.experimental import pallas as pl
from jax.experimental.pallas import tpu as pltpu
from jax.sharding import PartitionSpec as P

HEADS = 4
BLK = 128
NB = 4
META = 16
ROWS = 512
LOW = 32
MASKED = -1e30
LOG2E = 1.4426950408889634
VMEM_LIMIT = 24 * 1024 * 1024

epsilon = 1e-05

F32 = jnp.float32
BF16 = jnp.bfloat16


def dot(a, b):
    return jnp.dot(a, b, preferred_element_type=F32)


def dot_nt(a, b):
    return lax.dot_general(a, b, (((1,), (1,)), ((), ())), preferred_element_type=F32)


def silu(v):
    half = 0.5 * v
    return half + half * jnp.tanh(half)


def layer_norm(values, gains):
    average = jnp.mean(values, axis=-1, keepdims=True)
    centred = values - average
    spread_sq = jnp.mean(centred * centred, axis=-1, keepdims=True)
    return centred * lax.rsqrt(spread_sq + epsilon) * gains


class Held:
    def __init__(self, far, near, sem):
        self.near = near
        self.copy = pltpu.make_async_copy(far, near, sem)
        self.state = 0

    def start(self):
        if self.state == 0:
            self.copy.start()
            self.state = 1

    def __call__(self):
        self.start()
        if self.state == 1:
            self.copy.wait()
            self.state = 2
        return self.near


class Sent:
    def __init__(self, near, far, sem):
        self.near = near
        self.copy = pltpu.make_async_copy(near, far, sem)
        self.started = False

    def send(self):
        if not self.started:
            self.copy.start()
            self.started = True


def call(kernel, outs, args, kinds, scratch=(), late=(), flops=0, moved=0):
    n_in, n_out = len(args), len(outs)
    far_in = [i for i in range(n_in) if kinds[i] == "H"]
    far_out = [i for i in range(n_out) if outs[i][2] == "H"]

    def wrapped(*refs):
        ins, results = list(refs[:n_in]), list(refs[n_in : n_in + n_out])
        rest = list(refs[n_in + n_out :])
        sems = rest.pop(0)
        for n, i in enumerate(far_in):
            ins[i] = Held(ins[i], rest.pop(0), sems.at[n])
            if i not in late:
                ins[i].start()
        for n, i in enumerate(far_out):
            results[i] = Sent(rest.pop(0), results[i], sems.at[len(far_in) + n])
        kernel(*ins, *results, *rest)
        for i in far_out:
            results[i].send()
        for i in far_in:
            ins[i]()
        for i in far_out:
            results[i].copy.wait()

    spaces = {"V": pltpu.VMEM, "H": pltpu.HBM, "S": pltpu.SMEM}

    def spec(kind):
        return pl.BlockSpec(memory_space=pl.ANY if kind == "H" else spaces[kind])

    def placed(x, kind):
        return x if kind == "S" else pltpu.with_memory_space_constraint(x, spaces[kind])

    return pl.pallas_call(
        wrapped,
        out_shape=tuple(
            pltpu.HBM(shape, dtype) if kind == "H" else jax.ShapeDtypeStruct(shape, dtype)
            for shape, dtype, kind in outs
        ),
        in_specs=[spec(kind) for kind in kinds],
        out_specs=tuple(spec(kind) for _, _, kind in outs),
        scratch_shapes=[pltpu.SemaphoreType.DMA((max(1, len(far_in) + len(far_out)),))]
        + [pltpu.VMEM(args[i].shape, args[i].dtype) for i in far_in]
        + [pltpu.VMEM(outs[i][0], outs[i][1]) for i in far_out]
        + list(scratch),
        compiler_params=pltpu.CompilerParams(vmem_limit_bytes=VMEM_LIMIT),
        cost_estimate=pl.CostEstimate(flops=flops, bytes_accessed=moved, transcendentals=0),
    )(*[placed(x, kind) for x, kind in zip(args, kinds)])


def owner_onehot(owner, peers):
    places = lax.broadcasted_iota(jnp.int32, (peers, owner.shape[1]), 0)
    return jnp.where(places == owner, 1.0, 0.0).astype(F32)


def rank_onehot(rank, cap):
    places = lax.broadcasted_iota(jnp.int32, (cap, rank.shape[1]), 0).astype(F32)
    return jnp.where(places == rank, 1.0, 0.0).astype(BF16)


def bucket_kernel(peers, cap, weighted, turned, *refs):
    refs = list(refs)
    held_owner, held_slot = refs.pop(0), refs.pop(0)
    held_weight = refs.pop(0) if weighted else None
    held_rows = refs.pop(0)
    turns = [refs.pop(0) for _ in range(turned)]
    out, rank_out = refs.pop(0), refs.pop(0) if weighted else None
    turned_outs = [refs.pop(0) for _ in range(turned)]
    send_ref = out.near
    grid, width = held_rows.near.shape
    part = 256 if grid % 256 == 0 else grid
    upto = jnp.where(
        lax.broadcasted_iota(jnp.int32, (part, part), 0)
        <= lax.broadcasted_iota(jnp.int32, (part, part), 1),
        1.0,
        0.0,
    ).astype(BF16)
    owner = held_owner()[...]
    chosen = owner_onehot(owner, peers)
    chosen16 = chosen.astype(BF16)
    carry = jnp.zeros((peers, 1), F32)
    ranks = []
    for c in range(grid // part):
        span = slice(c * part, (c + 1) * part)
        counts = dot(chosen16[:, span], upto) + carry
        carry = counts[:, part - 1 :]
        ranks.append(jnp.sum(chosen[:, span] * counts, axis=0, keepdims=True) - 1.0)
    rank = jnp.concatenate(ranks, axis=1)
    if weighted:
        rank_out.near[...] = rank
    placed = rank_onehot(rank, cap)

    slots = held_slot()[...]
    pieces = [(slots // LOW).astype(F32), (slots % LOW).astype(F32)]
    if weighted:
        pieces.append(held_weight()[...])
    used = sum(p.shape[0] for p in pieces)
    pieces.append(jnp.zeros((META - used, grid), F32))
    features = jnp.concatenate(pieces, axis=0).astype(BF16).astype(F32)
    spread = (chosen[:, None, :] * features[None, :, :]).reshape(peers * META, grid)
    meta = dot_nt(spread.astype(BF16), placed).reshape(peers, META, cap)
    send_ref[:, cap:, :] = jnp.zeros((peers, META, width), BF16)
    send_ref[:, cap:, :cap] = meta.astype(BF16)

    rows = held_rows()[...]
    step = ROWS // cap
    for o in range(0, peers, step):
        select = (chosen16[o : o + step, None, :] * placed[None, :, :]).reshape(step * cap, grid)
        moved = dot(select, rows)
        send_ref[o : o + step, :cap, :] = moved.astype(BF16).reshape(step, cap, width)
    out.send()
    for f, t in zip(turns, turned_outs):
        source = f()
        skipped = source.shape[1] - t.near.shape[0]
        t.near[...] = source[:, skipped:].T
        t.send()


def bucket(owner, slots, weights, rows, turns, peers, cap):
    grid, width = rows.shape
    weighted = weights is not None
    args = (owner, slots) + ((weights,) if weighted else ()) + (rows,) + tuple(x for x, _ in turns)
    outs = [((peers, cap + META, width), BF16, "H")]
    if weighted:
        outs.append(((1, grid), F32, "H"))
    outs += [((count, x.shape[0]), x.dtype, "H") for x, count in turns]
    return call(
        functools.partial(bucket_kernel, peers, cap, weighted, len(turns)),
        outs,
        args,
        "H" * len(args),
        flops=2 * peers * cap * grid * width,
        moved=2 * (grid * width + peers * (cap + META) * width),
    )


def meta_row(got_ref, o, step, cap, row):
    return jnp.concatenate(
        [got_ref[r, cap:, :cap].astype(F32)[row : row + 1, :] for r in range(o, o + step)],
        axis=1,
    )


def slot_row(got_ref, o, step, cap, low, count):
    return meta_row(got_ref, o, step, cap, low) * LOW + meta_row(
        got_ref, o, step, cap, low + count
    )


def encode_kernel(peers, cap, got_ref, embed, message_w, state, gain, stream, normed, target_ref, message_ref):
    width = got_ref.shape[2]
    nodes = stream.near.shape[0]
    step = ROWS // cap
    places = lax.broadcasted_iota(jnp.int32, (nodes, ROWS), 0).astype(F32)
    starts = range(0, peers, step)
    for n, o in enumerate(starts):
        slot = slot_row(got_ref, o, step, cap, 0, 1)
        target_ref[:, n * ROWS : (n + 1) * ROWS] = jnp.where(places == slot, 1.0, 0.0).astype(BF16)
    embed_ref = embed()
    latents = [
        silu(dot(got_ref[o : o + step, :cap, :].reshape(ROWS, width), embed_ref[...])).astype(BF16)
        for o in starts
    ]
    message_w_ref = message_w()
    for n, latent in enumerate(latents):
        message_ref[n * ROWS : (n + 1) * ROWS, :] = dot(latent, message_w_ref[...]).astype(BF16)
    total = state()[...].astype(F32) + dot(target_ref[...], message_ref[...])
    normed.near[...] = layer_norm(total, gain()[0:1, :]).astype(BF16)
    normed.send()
    stream.near[...] = total


def layer_norm_columns(values, gains):
    average = jnp.mean(values, axis=0, keepdims=True)
    centred = values - average
    spread_sq = jnp.mean(centred * centred, axis=0, keepdims=True)
    return centred * lax.rsqrt(spread_sq + epsilon) * gains


def local_kernel(normed, qkv, value_t, stream, query_t, partial_t, stats, stream_t):
    width, nodes = query_t.near.shape
    head = width // HEADS
    rate = head ** (-0.5) * LOG2E
    held = normed()[...]
    qkv_ref = qkv()
    queries = dot(held, qkv_ref[:, :width]).astype(BF16).T
    query_t.near[...] = queries
    query_t.send()
    key = dot(held, qkv_ref[:, width : 2 * width]).astype(BF16)
    value = dot_nt(value_t()[...], held).astype(BF16)
    for h in range(HEADS):
        rows = slice(h * head, (h + 1) * head)
        scores = dot(key[:, rows], queries[rows, :])
        highest = jnp.max(scores, axis=0, keepdims=True)
        probs = jnp.exp2((scores - highest) * rate)
        stats.near[h : h + 1, :] = highest
        stats.near[HEADS + h : HEADS + h + 1, :] = jnp.sum(probs, axis=0, keepdims=True)
        partial_t.near[rows, :] = dot(value[rows, :], probs.astype(BF16))
    stats.send()
    partial_t.send()
    stream_t.near[...] = stream()[...].T


def tail_kernel(
    peers,
    cap,
    where_ref,
    att_ref,
    before_ref,
    after_ref,
    got_ref,
    qkv,
    value_t,
    query_t,
    stats,
    partial_t,
    stream_t,
    out_t,
    up_t,
    down_t,
    gain_t,
    embed_t,
    dec1_t,
    dec2_t,
    out_ref,
    key_ref,
    value_ref,
    attended_ref,
    mix_ref,
    hidden_ref,
):
    width, nodes = attended_ref.shape
    head = width // HEADS
    blocks = nodes // BLK
    rate = head ** (-0.5) * LOG2E
    has_before = where_ref[0] > 0
    has_after = where_ref[0] < where_ref[1] - 1
    step = ROWS // cap
    columns = got_ref.shape[2]
    chunks = list(enumerate(range(0, peers, step)))

    places = lax.broadcasted_iota(jnp.int32, (nodes, ROWS), 0).astype(F32)
    for n, o in chunks:
        mix = jnp.zeros((nodes, ROWS), F32)
        for k in range(3):
            slot = slot_row(got_ref, o, step, cap, k, 3)
            weight = meta_row(got_ref, o, step, cap, 6 + k)
            mix = mix + jnp.where(places == slot, weight, 0.0)
        mix_ref[n] = mix.astype(BF16)

    qkv_ref, value_t_ref = qkv(), value_t()
    for n, side in enumerate((before_ref, after_ref)):
        key_ref[n * nodes : (n + 1) * nodes, :] = dot(
            side[...], qkv_ref[:, width : 2 * width]
        ).astype(BF16)
        value = dot_nt(value_t_ref[...], side[...]).astype(BF16)
        for i in range(blocks):
            value_ref[n * blocks + i] = value[:, i * BLK : (i + 1) * BLK]

    query_ref, stats_ref, partial_ref = query_t(), stats(), partial_t()
    named = [[att_ref[i, k] for k in range(NB)] for i in range(blocks)]
    starts = [[pl.multiple_of(w * BLK, BLK) for w in row] for row in named]
    allowed = [
        [jnp.where(jnp.where(w < blocks, has_before, has_after), 0.0, MASKED) for w in row]
        for row in named
    ]
    for h in range(HEADS):
        rows = slice(h * head, (h + 1) * head)
        scores = []
        for i in range(blocks):
            queries = query_ref[rows, i * BLK : (i + 1) * BLK]
            keys = jnp.concatenate([key_ref[pl.ds(s, BLK), rows] for s in starts[i]], axis=0)
            found = dot(keys, queries)
            scores.append(
                jnp.concatenate(
                    [found[k * BLK : (k + 1) * BLK] + allowed[i][k] for k in range(NB)], axis=0
                )
            )
        scores = jnp.concatenate(scores, axis=1)
        held = stats_ref[h : h + 1, :]
        highest = jnp.maximum(held, jnp.max(scores, axis=0, keepdims=True))
        probs = jnp.exp2((scores - highest) * rate)
        keep = jnp.exp2((held - highest) * rate)
        totals = stats_ref[HEADS + h : HEADS + h + 1, :] * keep + jnp.sum(
            probs, axis=0, keepdims=True
        )
        weights = probs.astype(BF16)
        remote = []
        for i in range(blocks):
            values = jnp.concatenate([value_ref[w, rows, :] for w in named[i]], axis=1)
            remote.append(dot(values, weights[:, i * BLK : (i + 1) * BLK]))
        combined = partial_ref[rows, :] * keep + jnp.concatenate(remote, axis=1)
        attended_ref[rows, :] = (combined / totals).astype(BF16)

    gains = gain_t()[...]
    stream = stream_t()[...] + dot(out_t()[...], attended_ref[...])
    normed = layer_norm_columns(stream, gains[:, 1:2]).astype(BF16)
    up_ref = up_t()
    for c in range(0, up_ref.shape[0], width):
        hidden_ref[c : c + width, :] = silu(dot(up_ref[c : c + width, :], normed)).astype(BF16)
    stream = stream + dot(down_t()[...], hidden_ref[...])
    final = layer_norm_columns(stream, gains[:, 2:3]).astype(BF16)

    embed_ref, dec1_ref, dec2_ref = embed_t(), dec1_t(), dec2_t()
    latents = [
        silu(dot_nt(embed_ref[...], got_ref[o : o + step, :cap, :].reshape(ROWS, columns))).astype(
            BF16
        )
        for _, o in chunks
    ]
    pulled = [dot(final, mix_ref[n]).astype(BF16) for n, _ in chunks]
    mixed = [
        (latents[n].astype(F32) + pulled[n].astype(F32)).astype(BF16) for n, _ in chunks
    ]
    decoded = [silu(dot(dec1_ref[...], mixed[n])).astype(BF16) for n, _ in chunks]
    for n, o in chunks:
        result = dot(dec2_ref[...], decoded[n]).astype(BF16)
        for r in range(step):
            out_ref[o + r] = result[:, r * cap : (r + 1) * cap]


TAIL_KINDS = "SSVVVHHHHHHHHHHHHH"


def tail_scratch(nodes, width, slots, hidden):
    return (
        pltpu.VMEM((2 * nodes, width), BF16),
        pltpu.VMEM((2 * nodes // BLK, width, BLK), BF16),
        pltpu.VMEM((width, nodes), BF16),
        pltpu.VMEM((slots // ROWS, nodes, ROWS), BF16),
        pltpu.VMEM((hidden, nodes), BF16),
    )


def return_kernel(peers, cap, got_ref, rank, owner, out_ref):
    channels, grid = out_ref.shape
    placed = rank_onehot(rank[...], cap)
    chosen = owner_onehot(owner[...], peers)
    total = jnp.zeros((channels, grid), F32)
    for o in range(peers):
        total = total + dot(got_ref[o], placed) * chosen[o : o + 1, :]
    out_ref[...] = total.astype(BF16)


def body(
    grid_in,
    mesh_state,
    enc_owner,
    enc_slot,
    dec_owner,
    dec_slot,
    dec_weight,
    att_list,
    w_embed,
    w_message,
    norm_gain,
    w_qkv,
    w_out,
    w_up,
    w_down,
    w_dec1,
    w_dec2,
):
    peers = lax.axis_size("band")
    place = lax.axis_index("band")
    grid = grid_in.shape[0]
    nodes, width = mesh_state.shape
    cap = 2 * grid // peers
    channels = w_dec2.shape[1]
    slots = peers * cap

    def exchange(x):
        return lax.all_to_all(x, "band", split_axis=0, concat_axis=0, tiled=True)

    (enc_send,) = bucket(enc_owner.T, enc_slot.T, None, grid_in, (), peers, cap)
    enc_got = exchange(enc_send)
    dec_send, rank, embed_t, dec1_t, value_t, out_t, up_t, down_t = bucket(
        dec_owner.T,
        dec_slot.T,
        dec_weight.T,
        grid_in,
        (
            (w_embed, width),
            (w_dec1, width),
            (w_qkv[0], width),
            (w_out[0], width),
            (w_up[0], w_up.shape[2]),
            (w_down[0], width),
        ),
        peers,
        cap,
    )
    dec_got = exchange(dec_send)

    stream, normed = call(
        functools.partial(encode_kernel, peers, cap),
        (((nodes, width), F32, "H"), ((nodes, width), BF16, "H")),
        (enc_got, w_embed, w_message, mesh_state, norm_gain),
        "VHHHH",
        scratch=(pltpu.VMEM((nodes, slots), BF16), pltpu.VMEM((slots, width), BF16)),
        flops=2 * slots * width * (grid_in.shape[1] + width + nodes),
        moved=2 * slots * grid_in.shape[1] + 8 * nodes * width,
    )
    up = [(i, i + 1) for i in range(peers - 1)]
    down = [(j, i) for i, j in up]
    before = lax.ppermute(normed, "band", up)
    after = lax.ppermute(normed, "band", down)
    query_t, partial_t, stats, stream_t = call(
        local_kernel,
        (
            ((width, nodes), BF16, "H"),
            ((width, nodes), F32, "H"),
            ((2 * HEADS, nodes), F32, "H"),
            ((width, nodes), F32, "H"),
        ),
        (normed, w_qkv[0], value_t, stream),
        "HHHH",
        flops=2 * nodes * width * (3 * width + 2 * nodes),
        moved=2 * nodes * width * 8,
    )
    where = jnp.stack([place, jnp.int32(peers)]).astype(jnp.int32)
    (result,) = call(
        functools.partial(tail_kernel, peers, cap),
        (((peers, channels, cap), BF16, "V"),),
        (
            where,
            att_list,
            before,
            after,
            dec_got,
            w_qkv[0],
            value_t,
            query_t,
            stats,
            partial_t,
            stream_t,
            out_t,
            up_t,
            down_t,
            norm_gain.T,
            embed_t,
            dec1_t,
            w_dec2.T,
        ),
        TAIL_KINDS,
        scratch=tail_scratch(nodes, width, slots, w_up.shape[2]),
        flops=2 * nodes * width * (4 * width + 2 * nodes + width + 2 * w_up.shape[2])
        + 2 * slots * width * (grid_in.shape[1] + nodes + width + 128),
        moved=2 * width * (3 * width + width + 2 * w_up.shape[2]) + 10 * nodes * width,
    )
    returned = exchange(result)
    (denoised,) = call(
        functools.partial(return_kernel, peers, cap),
        (((channels, grid), BF16, "V"),),
        (returned, rank, dec_owner.T),
        "VVV",
        flops=2 * slots * channels * grid,
        moved=2 * slots * channels,
    )
    return denoised


def solution(mesh):
    return jax.shard_map(
        body,
        mesh=mesh,
        in_specs=(
            P(("ens", "band"), None),
            P("band", None),
            P("band", None),
            P("band", None),
            P("band", None),
            P("band", None),
            P("band", None),
            P("band", None),
            P(),
            P(),
            P(),
            P(),
            P(),
            P(),
            P(),
            P(),
            P(),
        ),
        out_specs=P(None, ("ens", "band")),
        check_vma=False,
    )
```

```python
import functools

import jax
import jax.numpy as jnp
from jax import lax
from jax.experimental import pallas as pl
from jax.experimental.pallas import tpu as pltpu
from jax.sharding import PartitionSpec as P

HEADS = 4
BLK = 128
NB = 4
META = 8
ROWS = 512
LOW = 128
UPPER = 4
KEYS_OF = 2
MASKED = -1e30
LOG2E = 1.4426950408889634
PARTS = 4
VMEM_LIMIT = 24 * 1024 * 1024

epsilon = 1e-05

F32 = jnp.float32
BF16 = jnp.bfloat16


def dot(a, b):
    return jnp.dot(a, b, preferred_element_type=F32)


def dot_nt(a, b):
    return lax.dot_general(a, b, (((1,), (1,)), ((), ())), preferred_element_type=F32)


def silu(v):
    half = 0.5 * v
    return half + half * jnp.tanh(half)


def layer_norm(values, gains):
    average = jnp.mean(values, axis=-1, keepdims=True)
    centred = values - average
    spread_sq = jnp.mean(centred * centred, axis=-1, keepdims=True)
    return centred * lax.rsqrt(spread_sq + epsilon) * gains


class Held:
    def __init__(self, far, near, sem):
        self.near = near
        self.copy = pltpu.make_async_copy(far, near, sem)
        self.state = 0

    def start(self):
        if self.state == 0:
            self.copy.start()
            self.state = 1

    def __call__(self):
        self.start()
        if self.state == 1:
            self.copy.wait()
            self.state = 2
        return self.near


class Near:
    def __init__(self, ref):
        self.near = ref

    def __call__(self):
        return self.near

    def send(self):
        pass


class Sent:
    def __init__(self, near, far, sem):
        self.near, self.far, self.sem = near, far, sem
        self.copies = []

    def send(self, n=0, part=None):
        near, far = (self.near, self.far) if part is None else (self.near.at[part], self.far.at[part])
        self.copies.append(pltpu.make_async_copy(near, far, self.sem.at[n]))
        self.copies[-1].start()

    def finish(self):
        for c in self.copies:
            c.wait()


def call(kernel, outs, args, kinds, scratch=(), late=(), flops=0, moved=0):
    n_in, n_out = len(args), len(outs)
    far_in = [i for i in range(n_in) if kinds[i] == "H"]
    far_out = [i for i in range(n_out) if outs[i][2] == "H"]

    def wrapped(*refs):
        ins, results = refs[:n_in], refs[n_in : n_in + n_out]
        rest = list(refs[n_in + n_out :])
        sems, out_sems = rest.pop(0), rest.pop(0)
        ins = [Near(r) if kinds[i] == "V" else r for i, r in enumerate(ins)]
        results = [Near(r) for r in results]
        for n, i in enumerate(far_in):
            ins[i] = Held(refs[i], rest.pop(0), sems.at[n])
            if i not in late:
                ins[i].start()
        for n, i in enumerate(far_out):
            results[i] = Sent(rest.pop(0), refs[n_in + i], out_sems.at[n])
        kernel(*ins, *results, *rest)
        for i in far_in:
            ins[i]()
        for i in far_out:
            if not results[i].copies:
                results[i].send()
        for i in far_out:
            results[i].finish()

    spaces = {"V": pltpu.VMEM, "H": pltpu.HBM, "S": pltpu.SMEM}

    def spec(kind):
        return pl.BlockSpec(memory_space=pl.ANY if kind == "H" else spaces[kind])

    def placed(x, kind):
        return x if kind == "S" else pltpu.with_memory_space_constraint(x, spaces[kind])

    return pl.pallas_call(
        wrapped,
        out_shape=tuple(
            pltpu.HBM(shape, dtype) if kind == "H" else jax.ShapeDtypeStruct(shape, dtype)
            for shape, dtype, kind in outs
        ),
        in_specs=[spec(kind) for kind in kinds],
        out_specs=tuple(spec(kind) for _, _, kind in outs),
        scratch_shapes=[
            pltpu.SemaphoreType.DMA((max(1, len(far_in)),)),
            pltpu.SemaphoreType.DMA((max(1, len(far_out)), PARTS)),
        ]
        + [pltpu.VMEM(args[i].shape, args[i].dtype) for i in far_in]
        + [pltpu.VMEM(outs[i][0], outs[i][1]) for i in far_out]
        + list(scratch),
        compiler_params=pltpu.CompilerParams(vmem_limit_bytes=VMEM_LIMIT),
        cost_estimate=pl.CostEstimate(flops=flops, bytes_accessed=moved, transcendentals=0),
    )(*[placed(x, kind) for x, kind in zip(args, kinds)])


def owner_onehot(owner, peers):
    places = lax.broadcasted_iota(jnp.int32, (peers, owner.shape[1]), 0)
    return jnp.where(places == owner, 1.0, 0.0).astype(F32)


def rank_onehot(rank, cap):
    places = lax.broadcasted_iota(jnp.int32, (cap, rank.shape[1]), 0).astype(F32)
    return jnp.where(places == rank, 1.0, 0.0).astype(BF16)


def bucket_kernel(peers, cap, weighted, turned, *refs):
    refs = list(refs)
    held_owner, held_slot = refs.pop(0), refs.pop(0)
    held_weight = refs.pop(0) if weighted else None
    held_rows = refs.pop(0)
    turns = [refs.pop(0) for _ in range(turned)]
    out = refs.pop(0)
    rank_out, key_out = (refs.pop(0), refs.pop(0)) if weighted else (None, None)
    turned_outs = [refs.pop(0) for _ in range(turned)]
    send_ref = out.near
    grid, width = held_rows.near.shape
    part = 256 if grid % 256 == 0 else grid
    upto = jnp.where(
        lax.broadcasted_iota(jnp.int32, (part, part), 0)
        <= lax.broadcasted_iota(jnp.int32, (part, part), 1),
        1.0,
        0.0,
    ).astype(BF16)
    owner = held_owner()[...]
    chosen = owner_onehot(owner, peers)
    chosen16 = chosen.astype(BF16)
    carry = jnp.zeros((peers, 1), F32)
    ranks = []
    for c in range(grid // part):
        span = slice(c * part, (c + 1) * part)
        counts = dot(chosen16[:, span], upto) + carry
        carry = counts[:, part - 1 :]
        ranks.append(jnp.sum(chosen[:, span] * counts, axis=0, keepdims=True) - 1.0)
    rank = jnp.concatenate(ranks, axis=1)
    if weighted:
        rank_out.near[...] = rank
    placed = rank_onehot(rank, cap)

    slots = held_slot()[...]
    lower = lax.rem(slots, LOW)
    upper = lax.div(slots, LOW)
    packed = upper[0:1]
    for k in range(1, slots.shape[0]):
        packed = packed + upper[k : k + 1] * UPPER**k
    pieces = [lower.astype(F32), packed.astype(F32)]
    if weighted:
        pieces.append(held_weight()[...])
    used = sum(p.shape[0] for p in pieces)
    if used < META:
        pieces.append(jnp.zeros((META - used, grid), F32))
    features = jnp.concatenate(pieces, axis=0).astype(BF16).astype(F32)
    spread = (chosen[:, None, :] * features[None, :, :]).reshape(peers * META, grid)
    meta = dot_nt(spread.astype(BF16), placed).reshape(peers, META, cap)
    send_ref[:, cap:, :] = jnp.zeros((peers, META, width), BF16)
    send_ref[:, cap:, :cap] = meta.astype(BF16)

    rows = held_rows()[...]
    step = ROWS // cap
    for n, o in enumerate(range(0, peers, step)):
        select = (chosen16[o : o + step, None, :] * placed[None, :, :]).reshape(step * cap, grid)
        moved = dot(select, rows)
        send_ref[o : o + step, :cap, :] = moved.astype(BF16).reshape(step, cap, width)
        out.send(n, pl.ds(o, step))
    for f, t in zip(turns, turned_outs):
        source = f()
        skipped = source.shape[1] - t.near.shape[0]
        t.near[...] = source[:, skipped:].T
        t.send()
    if weighted:
        columns = key_out.near.shape[1]
        key_out.near[...] = turns[KEYS_OF]()[:, columns : 2 * columns]


def bucket(owner, slots, weights, rows, turns, peers, cap):
    grid, width = rows.shape
    weighted = weights is not None
    args = (owner, slots) + ((weights,) if weighted else ()) + (rows,) + tuple(x for x, _ in turns)
    outs = [((peers, cap + META, width), BF16, "H")]
    if weighted:
        depth, columns = turns[KEYS_OF][0].shape
        outs += [((1, grid), F32, "H"), ((depth, columns // 3), BF16, "H")]
    outs += [((count, x.shape[0]), x.dtype, "H") for x, count in turns]
    return call(
        functools.partial(bucket_kernel, peers, cap, weighted, len(turns)),
        outs,
        args,
        "H" * len(args),
        flops=2 * peers * cap * grid * width,
        moved=2 * (grid * width + peers * (cap + META) * width),
    )


def meta_row(got_ref, o, step, cap, row):
    return jnp.concatenate(
        [got_ref[r, cap:, :cap].astype(F32)[row : row + 1, :] for r in range(o, o + step)],
        axis=1,
    )


def slot_rows(got_ref, o, step, cap, count):
    upper = meta_row(got_ref, o, step, cap, count).astype(jnp.int32)
    rows = []
    for k in range(count):
        rows.append(
            meta_row(got_ref, o, step, cap, k)
            + (lax.rem(lax.div(upper, UPPER**k), UPPER) * LOW).astype(F32)
        )
    return rows


def encode_kernel(peers, cap, got, embed, message_w, state, gain, stream, normed, target_ref, message_ref):
    got_ref = got()
    width = got_ref.shape[2]
    nodes = stream.near.shape[0]
    step = ROWS // cap
    places = lax.broadcasted_iota(jnp.int32, (nodes, ROWS), 0).astype(F32)
    starts = range(0, peers, step)
    for n, o in enumerate(starts):
        (slot,) = slot_rows(got_ref, o, step, cap, 1)
        target_ref[:, n * ROWS : (n + 1) * ROWS] = jnp.where(places == slot, 1.0, 0.0).astype(BF16)
    embed_ref = embed()
    latents = [
        silu(dot(got_ref[o : o + step, :cap, :].reshape(ROWS, width), embed_ref[...])).astype(BF16)
        for o in starts
    ]
    message_w_ref = message_w()
    for n, latent in enumerate(latents):
        message_ref[n * ROWS : (n + 1) * ROWS, :] = dot(latent, message_w_ref[...]).astype(BF16)
    total = state()[...].astype(F32) + dot(target_ref[...], message_ref[...])
    stream.near[...] = total
    stream.send()
    normed.near[...] = layer_norm(total, gain()[0:1, :]).astype(BF16)


def layer_norm_columns(values, gains):
    average = jnp.mean(values, axis=0, keepdims=True)
    centred = values - average
    spread_sq = jnp.mean(centred * centred, axis=0, keepdims=True)
    return centred * lax.rsqrt(spread_sq + epsilon) * gains


def local_kernel(normed, qkv, value_t, stream, query_t, partial_t, stats, stream_t):
    width, nodes = query_t.near.shape
    head = width // HEADS
    rate = head ** (-0.5) * LOG2E
    held = normed()[...]
    qkv_ref = qkv()
    queries = dot(held, qkv_ref[:, :width]).astype(BF16).T
    query_t.near[...] = queries
    query_t.send()
    key = dot(held, qkv_ref[:, width : 2 * width]).astype(BF16)
    value = dot_nt(value_t()[...], held).astype(BF16)
    for h in range(HEADS):
        rows = slice(h * head, (h + 1) * head)
        scores = dot(key[:, rows], queries[rows, :])
        highest = jnp.max(scores, axis=0, keepdims=True)
        probs = jnp.exp2((scores - highest) * rate)
        stats.near[h : h + 1, :] = highest
        stats.near[HEADS + h : HEADS + h + 1, :] = jnp.sum(probs, axis=0, keepdims=True)
        partial_t.near[rows, :] = dot(value[rows, :], probs.astype(BF16))
    stats.send()
    partial_t.send()
    stream_t.near[...] = stream()[...].T


def tail_kernel(
    peers,
    cap,
    where_ref,
    att_ref,
    before,
    after,
    got,
    embed_t,
    key_w,
    value_t,
    query_t,
    stats,
    partial_t,
    stream_t,
    out_t,
    up_t,
    down_t,
    gain_t,
    dec1_t,
    dec2_t,
    out,
    key_ref,
    value_ref,
    attended_ref,
    mix_ref,
    hidden_ref,
):
    before_ref, after_ref, got_ref, out_ref = before(), after(), got(), out.near
    width, nodes = attended_ref.shape
    head = width // HEADS
    blocks = nodes // BLK
    rate = head ** (-0.5) * LOG2E
    has_before = where_ref[0] > 0
    has_after = where_ref[0] < where_ref[1] - 1
    step = ROWS // cap
    columns = got_ref.shape[2]
    chunks = list(enumerate(range(0, peers, step)))

    places = lax.broadcasted_iota(jnp.int32, (nodes, ROWS), 0).astype(F32)
    for n, o in chunks:
        mix = jnp.zeros((nodes, ROWS), F32)
        for k, slot in enumerate(slot_rows(got_ref, o, step, cap, 3)):
            weight = meta_row(got_ref, o, step, cap, 4 + k)
            mix = mix + jnp.where(places == slot, weight, 0.0)
        mix_ref[n] = mix.astype(BF16)

    embed_ref = embed_t()
    latents = [
        silu(dot_nt(embed_ref[...], got_ref[o : o + step, :cap, :].reshape(ROWS, columns))).astype(
            BF16
        )
        for _, o in chunks
    ]

    key_w_ref, value_t_ref = key_w(), value_t()
    for n, side in enumerate((before_ref, after_ref)):
        key_ref[n * nodes : (n + 1) * nodes, :] = dot(side[...], key_w_ref[...]).astype(
            BF16
        )
        value = dot_nt(value_t_ref[...], side[...]).astype(BF16)
        for i in range(blocks):
            value_ref[n * blocks + i] = value[:, i * BLK : (i + 1) * BLK]

    query_ref, stats_ref, partial_ref = query_t(), stats(), partial_t()
    named = [[att_ref[i, k] for k in range(NB)] for i in range(blocks)]
    starts = [[pl.multiple_of(w * BLK, BLK) for w in row] for row in named]
    allowed = [
        [jnp.where(jnp.where(w < blocks, has_before, has_after), 0.0, MASKED) for w in row]
        for row in named
    ]
    for h in range(HEADS):
        rows = slice(h * head, (h + 1) * head)
        scores = []
        for i in range(blocks):
            queries = query_ref[rows, i * BLK : (i + 1) * BLK]
            keys = jnp.concatenate([key_ref[pl.ds(s, BLK), rows] for s in starts[i]], axis=0)
            found = dot(keys, queries)
            scores.append(
                jnp.concatenate(
                    [found[k * BLK : (k + 1) * BLK] + allowed[i][k] for k in range(NB)], axis=0
                )
            )
        scores = jnp.concatenate(scores, axis=1)
        held = stats_ref[h : h + 1, :]
        highest = jnp.maximum(held, jnp.max(scores, axis=0, keepdims=True))
        probs = jnp.exp2((scores - highest) * rate)
        keep = jnp.exp2((held - highest) * rate)
        totals = stats_ref[HEADS + h : HEADS + h + 1, :] * keep + jnp.sum(
            probs, axis=0, keepdims=True
        )
        weights = probs.astype(BF16)
        remote = []
        for i in range(blocks):
            values = jnp.concatenate([value_ref[w, rows, :] for w in named[i]], axis=1)
            remote.append(dot(values, weights[:, i * BLK : (i + 1) * BLK]))
        combined = partial_ref[rows, :] * keep + jnp.concatenate(remote, axis=1)
        attended_ref[rows, :] = (combined / totals).astype(BF16)

    gains = gain_t()[...]
    stream = stream_t()[...] + dot(out_t()[...], attended_ref[...])
    normed = layer_norm_columns(stream, gains[:, 1:2]).astype(BF16)
    up_ref = up_t()
    for c in range(0, up_ref.shape[0], width):
        hidden_ref[c : c + width, :] = silu(dot(up_ref[c : c + width, :], normed)).astype(BF16)
    stream = stream + dot(down_t()[...], hidden_ref[...])
    final = layer_norm_columns(stream, gains[:, 2:3]).astype(BF16)

    dec1_ref, dec2_ref = dec1_t(), dec2_t()
    pulled = [dot(final, mix_ref[n]).astype(BF16) for n, _ in chunks]
    mixed = [
        (latents[n].astype(F32) + pulled[n].astype(F32)).astype(BF16) for n, _ in chunks
    ]
    decoded = [silu(dot(dec1_ref[...], mixed[n])).astype(BF16) for n, _ in chunks]
    for n, o in chunks:
        result = dot(dec2_ref[...], decoded[n]).astype(BF16)
        for r in range(step):
            out_ref[o + r] = result[:, r * cap : (r + 1) * cap]


TAIL_KINDS = "SSVVVHHHHHHHHHHHHH"


def tail_scratch(nodes, width, slots, hidden):
    return (
        pltpu.VMEM((2 * nodes, width), BF16),
        pltpu.VMEM((2 * nodes // BLK, width, BLK), BF16),
        pltpu.VMEM((width, nodes), BF16),
        pltpu.VMEM((slots // ROWS, nodes, ROWS), BF16),
        pltpu.VMEM((hidden, nodes), BF16),
    )


def return_kernel(peers, cap, got, rank, owner, out):
    channels, grid = out.near.shape
    placed = rank_onehot(rank()[...], cap)
    chosen = owner_onehot(owner()[...], peers)
    total = jnp.zeros((channels, grid), F32)
    for o in range(peers):
        total = total + dot(got()[o], placed) * chosen[o : o + 1, :]
    out.near[...] = total.astype(BF16)


def body(
    grid_in,
    mesh_state,
    enc_owner,
    enc_slot,
    dec_owner,
    dec_slot,
    dec_weight,
    att_list,
    w_embed,
    w_message,
    norm_gain,
    w_qkv,
    w_out,
    w_up,
    w_down,
    w_dec1,
    w_dec2,
):
    peers = lax.axis_size("band")
    place = lax.axis_index("band")
    grid = grid_in.shape[0]
    nodes, width = mesh_state.shape
    cap = 2 * grid // peers
    channels = w_dec2.shape[1]
    slots = peers * cap

    def exchange(x):
        return lax.all_to_all(x, "band", split_axis=0, concat_axis=0, tiled=True)

    (enc_send,) = bucket(enc_owner.T, enc_slot.T, None, grid_in, (), peers, cap)
    enc_got = exchange(enc_send)
    dec_send, rank, key_w, embed_t, dec1_t, value_t, out_t, up_t, down_t = bucket(
        dec_owner.T,
        dec_slot.T,
        dec_weight.T,
        grid_in,
        (
            (w_embed, width),
            (w_dec1, width),
            (w_qkv[0], width),
            (w_out[0], width),
            (w_up[0], w_up.shape[2]),
            (w_down[0], width),
        ),
        peers,
        cap,
    )
    dec_got = exchange(dec_send)

    stream, normed = call(
        functools.partial(encode_kernel, peers, cap),
        (((nodes, width), F32, "H"), ((nodes, width), BF16, "H")),
        (enc_got, w_embed, w_message, mesh_state, norm_gain),
        "VHHHH",
        scratch=(pltpu.VMEM((nodes, slots), BF16), pltpu.VMEM((slots, width), BF16)),
        flops=2 * slots * width * (grid_in.shape[1] + width + nodes),
        moved=2 * slots * grid_in.shape[1] + 8 * nodes * width,
    )
    up = [(i, i + 1) for i in range(peers - 1)]
    down = [(j, i) for i, j in up]
    before = lax.ppermute(normed, "band", up)
    after = lax.ppermute(normed, "band", down)
    query_t, partial_t, stats, stream_t = call(
        local_kernel,
        (
            ((width, nodes), BF16, "H"),
            ((width, nodes), F32, "H"),
            ((2 * HEADS, nodes), F32, "H"),
            ((width, nodes), F32, "H"),
        ),
        (normed, w_qkv[0], value_t, stream),
        "HHHH",
        flops=2 * nodes * width * (3 * width + 2 * nodes),
        moved=2 * nodes * width * 8,
    )
    where = jnp.stack([place, jnp.int32(peers)]).astype(jnp.int32)
    (result,) = call(
        functools.partial(tail_kernel, peers, cap),
        (((peers, channels, cap), BF16, "V"),),
        (
            where,
            att_list,
            before,
            after,
            dec_got,
            embed_t,
            key_w,
            value_t,
            query_t,
            stats,
            partial_t,
            stream_t,
            out_t,
            up_t,
            down_t,
            norm_gain.T,
            dec1_t,
            w_dec2.T,
        ),
        TAIL_KINDS,
        scratch=tail_scratch(nodes, width, slots, w_up.shape[2]),
        flops=2 * nodes * width * (4 * width + 2 * nodes + width + 2 * w_up.shape[2])
        + 2 * slots * width * (grid_in.shape[1] + nodes + width + 128),
        moved=2 * width * (3 * width + width + 2 * w_up.shape[2]) + 10 * nodes * width,
    )
    returned = exchange(result)
    (denoised,) = call(
        functools.partial(return_kernel, peers, cap),
        (((channels, grid), BF16, "V"),),
        (returned, rank, dec_owner.T),
        "VVV",
        flops=2 * slots * channels * grid,
        moved=2 * slots * channels,
    )
    return denoised


def solution(mesh):
    return jax.shard_map(
        body,
        mesh=mesh,
        in_specs=(
            P(("ens", "band"), None),
            P("band", None),
            P("band", None),
            P("band", None),
            P("band", None),
            P("band", None),
            P("band", None),
            P("band", None),
            P(),
            P(),
            P(),
            P(),
            P(),
            P(),
            P(),
            P(),
            P(),
        ),
        out_specs=P(None, ("ens", "band")),
        check_vma=False,
    )
```

```python
import functools

import jax
import jax.numpy as jnp
from jax import lax
from jax.experimental import pallas as pl
from jax.experimental.pallas import tpu as pltpu
from jax.sharding import PartitionSpec as P

HEADS = 4
BLK = 128
NB = 4
META = 8
ROWS = 512
LOW = 128
UPPER = 4
KEYS_OF = 2
MASKED = -1e30
LOG2E = 1.4426950408889634
PARTS = 4
VMEM_LIMIT = 24 * 1024 * 1024

epsilon = 1e-05

F32 = jnp.float32
BF16 = jnp.bfloat16


def dot(a, b):
    return jnp.dot(a, b, preferred_element_type=F32)


def dot_nt(a, b):
    return lax.dot_general(a, b, (((1,), (1,)), ((), ())), preferred_element_type=F32)


def silu(v):
    half = 0.5 * v
    return half + half * jnp.tanh(half)


def layer_norm(values, gains):
    average = jnp.mean(values, axis=-1, keepdims=True)
    centred = values - average
    spread_sq = jnp.mean(centred * centred, axis=-1, keepdims=True)
    return centred * lax.rsqrt(spread_sq + epsilon) * gains


class Held:
    def __init__(self, far, near, sem):
        self.near = near
        self.copy = pltpu.make_async_copy(far, near, sem)
        self.state = 0

    def start(self):
        if self.state == 0:
            self.copy.start()
            self.state = 1

    def __call__(self):
        self.start()
        if self.state == 1:
            self.copy.wait()
            self.state = 2
        return self.near


class Near:
    def __init__(self, ref):
        self.near = ref

    def __call__(self):
        return self.near

    def send(self):
        pass


class Sent:
    def __init__(self, near, far, sem):
        self.near, self.far, self.sem = near, far, sem
        self.copies = []

    def send(self, n=0, part=None):
        near, far = (self.near, self.far) if part is None else (self.near.at[part], self.far.at[part])
        self.copies.append(pltpu.make_async_copy(near, far, self.sem.at[n]))
        self.copies[-1].start()

    def finish(self):
        for c in self.copies:
            c.wait()


def call(kernel, outs, args, kinds, scratch=(), late=(), flops=0, moved=0):
    n_in, n_out = len(args), len(outs)
    far_in = [i for i in range(n_in) if kinds[i] == "H"]
    far_out = [i for i in range(n_out) if outs[i][2] == "H"]

    def wrapped(*refs):
        ins, results = refs[:n_in], refs[n_in : n_in + n_out]
        rest = list(refs[n_in + n_out :])
        sems, out_sems = rest.pop(0), rest.pop(0)
        ins = [Near(r) if kinds[i] == "V" else r for i, r in enumerate(ins)]
        results = [Near(r) for r in results]
        for n, i in enumerate(far_in):
            ins[i] = Held(refs[i], rest.pop(0), sems.at[n])
            if i not in late:
                ins[i].start()
        for n, i in enumerate(far_out):
            results[i] = Sent(rest.pop(0), refs[n_in + i], out_sems.at[n])
        kernel(*ins, *results, *rest)
        for i in far_in:
            ins[i]()
        for i in far_out:
            if not results[i].copies:
                results[i].send()
        for i in far_out:
            results[i].finish()

    spaces = {"V": pltpu.VMEM, "H": pltpu.HBM, "R": pltpu.HBM, "S": pltpu.SMEM}

    def spec(kind):
        return pl.BlockSpec(memory_space=pl.ANY if kind in "HR" else spaces[kind])

    def placed(x, kind):
        return x if kind == "S" else pltpu.with_memory_space_constraint(x, spaces[kind])

    return pl.pallas_call(
        wrapped,
        out_shape=tuple(
            pltpu.HBM(shape, dtype) if kind == "H" else jax.ShapeDtypeStruct(shape, dtype)
            for shape, dtype, kind in outs
        ),
        in_specs=[spec(kind) for kind in kinds],
        out_specs=tuple(spec(kind) for _, _, kind in outs),
        scratch_shapes=[
            pltpu.SemaphoreType.DMA((max(1, len(far_in)),)),
            pltpu.SemaphoreType.DMA((max(1, len(far_out)), PARTS)),
        ]
        + [pltpu.VMEM(args[i].shape, args[i].dtype) for i in far_in]
        + [pltpu.VMEM(outs[i][0], outs[i][1]) for i in far_out]
        + list(scratch),
        compiler_params=pltpu.CompilerParams(vmem_limit_bytes=VMEM_LIMIT),
        cost_estimate=pl.CostEstimate(flops=flops, bytes_accessed=moved, transcendentals=0),
    )(*[placed(x, kind) for x, kind in zip(args, kinds)])


def owner_onehot(owner, peers):
    places = lax.broadcasted_iota(jnp.int32, (peers, owner.shape[1]), 0)
    return jnp.where(places == owner, 1.0, 0.0).astype(F32)


def rank_onehot(rank, cap):
    places = lax.broadcasted_iota(jnp.int32, (cap, rank.shape[1]), 0).astype(F32)
    return jnp.where(places == rank, 1.0, 0.0).astype(BF16)


def bucket_kernel(peers, cap, weighted, turned, *refs):
    refs = list(refs)
    held_owner, held_slot = refs.pop(0), refs.pop(0)
    held_weight = refs.pop(0) if weighted else None
    held_rows = refs.pop(0)
    turns = [refs.pop(0) for _ in range(turned)]
    out = refs.pop(0)
    rank_out, key_out = (refs.pop(0), refs.pop(0)) if weighted else (None, None)
    turned_outs = [refs.pop(0) for _ in range(turned)]
    send_ref = out.near
    grid, width = held_rows.near.shape
    part = 256 if grid % 256 == 0 else grid
    upto = jnp.where(
        lax.broadcasted_iota(jnp.int32, (part, part), 0)
        <= lax.broadcasted_iota(jnp.int32, (part, part), 1),
        1.0,
        0.0,
    ).astype(BF16)
    owner = held_owner()[...]
    chosen = owner_onehot(owner, peers)
    chosen16 = chosen.astype(BF16)
    carry = jnp.zeros((peers, 1), F32)
    ranks = []
    for c in range(grid // part):
        span = slice(c * part, (c + 1) * part)
        counts = dot(chosen16[:, span], upto) + carry
        carry = counts[:, part - 1 :]
        ranks.append(jnp.sum(chosen[:, span] * counts, axis=0, keepdims=True) - 1.0)
    rank = jnp.concatenate(ranks, axis=1)
    if weighted:
        rank_out.near[...] = rank
    placed = rank_onehot(rank, cap)

    slots = held_slot()[...]
    lower = lax.rem(slots, LOW)
    upper = lax.div(slots, LOW)
    packed = upper[0:1]
    for k in range(1, slots.shape[0]):
        packed = packed + upper[k : k + 1] * UPPER**k
    pieces = [lower.astype(F32), packed.astype(F32)]
    if weighted:
        pieces.append(held_weight()[...])
    used = sum(p.shape[0] for p in pieces)
    if used < META:
        pieces.append(jnp.zeros((META - used, grid), F32))
    features = jnp.concatenate(pieces, axis=0).astype(BF16).astype(F32)
    spread = (chosen[:, None, :] * features[None, :, :]).reshape(peers * META, grid)
    meta = dot_nt(spread.astype(BF16), placed).reshape(peers, META, cap)
    send_ref[:, cap:, :] = jnp.zeros((peers, META, width), BF16)
    send_ref[:, cap:, :cap] = meta.astype(BF16)

    rows = held_rows()[...]
    step = ROWS // cap
    for n, o in enumerate(range(0, peers, step)):
        select = (chosen16[o : o + step, None, :] * placed[None, :, :]).reshape(step * cap, grid)
        moved = dot(select, rows)
        send_ref[o : o + step, :cap, :] = moved.astype(BF16).reshape(step, cap, width)
        out.send(n, pl.ds(o, step))
    for f, t in zip(turns, turned_outs):
        source = f()
        skipped = source.shape[1] - t.near.shape[0]
        t.near[...] = source[:, skipped:].T
        t.send()
    if weighted:
        columns = key_out.near.shape[1]
        key_out.near[...] = turns[KEYS_OF]()[:, columns : 2 * columns]


def bucket(owner, slots, weights, rows, turns, peers, cap):
    grid, width = rows.shape
    weighted = weights is not None
    args = (owner, slots) + ((weights,) if weighted else ()) + (rows,) + tuple(x for x, _ in turns)
    outs = [((peers, cap + META, width), BF16, "H")]
    if weighted:
        depth, columns = turns[KEYS_OF][0].shape
        outs += [((1, grid), F32, "H"), ((depth, columns // 3), BF16, "H")]
    outs += [((count, x.shape[0]), x.dtype, "H") for x, count in turns]
    return call(
        functools.partial(bucket_kernel, peers, cap, weighted, len(turns)),
        outs,
        args,
        "H" * len(args),
        flops=2 * peers * cap * grid * width,
        moved=2 * (grid * width + peers * (cap + META) * width),
    )


def meta_row(got_ref, o, step, cap, row):
    return jnp.concatenate(
        [got_ref[r, cap:, :cap].astype(F32)[row : row + 1, :] for r in range(o, o + step)],
        axis=1,
    )


def slot_rows(got_ref, o, step, cap, count):
    upper = meta_row(got_ref, o, step, cap, count).astype(jnp.int32)
    rows = []
    for k in range(count):
        rows.append(
            meta_row(got_ref, o, step, cap, k)
            + (lax.rem(lax.div(upper, UPPER**k), UPPER) * LOW).astype(F32)
        )
    return rows


def encode_kernel(peers, cap, got, embed, message_w, state, gain, stream, normed, target_ref, message_ref):
    got_ref = got()
    width = got_ref.shape[2]
    nodes = stream.near.shape[0]
    step = ROWS // cap
    places = lax.broadcasted_iota(jnp.int32, (nodes, ROWS), 0).astype(F32)
    starts = range(0, peers, step)
    for n, o in enumerate(starts):
        (slot,) = slot_rows(got_ref, o, step, cap, 1)
        target_ref[:, n * ROWS : (n + 1) * ROWS] = jnp.where(places == slot, 1.0, 0.0).astype(BF16)
    embed_ref = embed()
    latents = [
        silu(dot(got_ref[o : o + step, :cap, :].reshape(ROWS, width), embed_ref[...])).astype(BF16)
        for o in starts
    ]
    message_w_ref = message_w()
    for n, latent in enumerate(latents):
        message_ref[n * ROWS : (n + 1) * ROWS, :] = dot(latent, message_w_ref[...]).astype(BF16)
    total = state()[...].astype(F32) + dot(target_ref[...], message_ref[...])
    stream.near[...] = total
    stream.send()
    normed.near[...] = layer_norm(total, gain()[0:1, :]).astype(BF16)


def layer_norm_columns(values, gains):
    average = jnp.mean(values, axis=0, keepdims=True)
    centred = values - average
    spread_sq = jnp.mean(centred * centred, axis=0, keepdims=True)
    return centred * lax.rsqrt(spread_sq + epsilon) * gains


def local_kernel(normed, qkv, value_t, stream, query_t, partial_t, stats, stream_t):
    width, nodes = query_t.near.shape
    head = width // HEADS
    rate = head ** (-0.5) * LOG2E
    held = normed()[...]
    qkv_ref = qkv()
    queries = dot(held, qkv_ref[:, :width]).astype(BF16).T
    query_t.near[...] = queries
    query_t.send()
    key = dot(held, qkv_ref[:, width : 2 * width]).astype(BF16)
    value = dot_nt(value_t()[...], held).astype(BF16)
    for h in range(HEADS):
        rows = slice(h * head, (h + 1) * head)
        scores = dot(key[:, rows], queries[rows, :])
        highest = jnp.max(scores, axis=0, keepdims=True)
        probs = jnp.exp2((scores - highest) * rate)
        stats.near[h : h + 1, :] = highest
        stats.near[HEADS + h : HEADS + h + 1, :] = jnp.sum(probs, axis=0, keepdims=True)
        partial_t.near[rows, :] = dot(value[rows, :], probs.astype(BF16))
    stats.send()
    partial_t.send()
    stream_t.near[...] = stream()[...].T


def request_kernel(peers, cap, got, embed_t, *refs):
    carried = (len(refs) - 3) // 2
    sources, (mix, latent) = refs[:carried], refs[carried : carried + 2]
    targets, sems = refs[carried + 2 : -1], refs[-1]
    copies = [
        pltpu.make_async_copy(f, t.near, sems.at[n])
        for n, (f, t) in enumerate(zip(sources, targets))
    ]
    for c in copies:
        c.start()
    got_ref, mix_ref, latent_ref = got(), mix.near, latent.near
    nodes = mix_ref.shape[1]
    columns = got_ref.shape[2]
    step = ROWS // cap
    chunks = list(enumerate(range(0, peers, step)))

    places = lax.broadcasted_iota(jnp.int32, (nodes, ROWS), 0).astype(F32)
    for n, o in chunks:
        mix = jnp.zeros((nodes, ROWS), F32)
        for k, slot in enumerate(slot_rows(got_ref, o, step, cap, 3)):
            weight = meta_row(got_ref, o, step, cap, 4 + k)
            mix = mix + jnp.where(places == slot, weight, 0.0)
        mix_ref[n] = mix.astype(BF16)

    embed_ref = embed_t()
    for n, o in chunks:
        rows = got_ref[o : o + step, :cap, :].reshape(ROWS, columns)
        latent_ref[n] = silu(dot_nt(embed_ref[...], rows)).astype(BF16)
    for c in copies:
        c.wait()


def tail_kernel(
    peers,
    cap,
    where_ref,
    att_ref,
    before,
    after,
    mix,
    latent,
    key_w,
    value_t,
    query_t,
    stats,
    partial_t,
    stream_t,
    out_t,
    up_t,
    down_t,
    dec1_t,
    gain_t,
    dec2_t,
    out,
    key_ref,
    value_ref,
    attended_ref,
    hidden_ref,
):
    before_ref, after_ref, out_ref = before(), after(), out.near
    mix_ref, latent_ref = mix(), latent()
    width, nodes = attended_ref.shape
    head = width // HEADS
    blocks = nodes // BLK
    rate = head ** (-0.5) * LOG2E
    has_before = where_ref[0] > 0
    has_after = where_ref[0] < where_ref[1] - 1
    step = ROWS // cap
    chunks = list(enumerate(range(0, peers, step)))

    key_w_ref, value_t_ref = key_w(), value_t()
    for n, side in enumerate((before_ref, after_ref)):
        key_ref[n * nodes : (n + 1) * nodes, :] = dot(side[...], key_w_ref[...]).astype(
            BF16
        )
        value = dot_nt(value_t_ref[...], side[...]).astype(BF16)
        for i in range(blocks):
            value_ref[n * blocks + i] = value[:, i * BLK : (i + 1) * BLK]

    query_ref, stats_ref, partial_ref = query_t(), stats(), partial_t()
    named = [[att_ref[i, k] for k in range(NB)] for i in range(blocks)]
    starts = [[pl.multiple_of(w * BLK, BLK) for w in row] for row in named]
    allowed = [
        [jnp.where(jnp.where(w < blocks, has_before, has_after), 0.0, MASKED) for w in row]
        for row in named
    ]
    for h in range(HEADS):
        rows = slice(h * head, (h + 1) * head)
        scores = []
        for i in range(blocks):
            queries = query_ref[rows, i * BLK : (i + 1) * BLK]
            keys = jnp.concatenate([key_ref[pl.ds(s, BLK), rows] for s in starts[i]], axis=0)
            found = dot(keys, queries)
            scores.append(
                jnp.concatenate(
                    [found[k * BLK : (k + 1) * BLK] + allowed[i][k] for k in range(NB)], axis=0
                )
            )
        scores = jnp.concatenate(scores, axis=1)
        held = stats_ref[h : h + 1, :]
        highest = jnp.maximum(held, jnp.max(scores, axis=0, keepdims=True))
        probs = jnp.exp2((scores - highest) * rate)
        keep = jnp.exp2((held - highest) * rate)
        totals = stats_ref[HEADS + h : HEADS + h + 1, :] * keep + jnp.sum(
            probs, axis=0, keepdims=True
        )
        weights = probs.astype(BF16)
        remote = []
        for i in range(blocks):
            values = jnp.concatenate([value_ref[w, rows, :] for w in named[i]], axis=1)
            remote.append(dot(values, weights[:, i * BLK : (i + 1) * BLK]))
        combined = partial_ref[rows, :] * keep + jnp.concatenate(remote, axis=1)
        attended_ref[rows, :] = (combined / totals).astype(BF16)

    gains = gain_t()[...]
    stream = stream_t()[...] + dot(out_t()[...], attended_ref[...])
    normed = layer_norm_columns(stream, gains[:, 1:2]).astype(BF16)
    up_ref = up_t()
    for c in range(0, up_ref.shape[0], width):
        hidden_ref[c : c + width, :] = silu(dot(up_ref[c : c + width, :], normed)).astype(BF16)
    stream = stream + dot(down_t()[...], hidden_ref[...])
    final = layer_norm_columns(stream, gains[:, 2:3]).astype(BF16)

    dec1_ref, dec2_ref = dec1_t(), dec2_t()
    pulled = [dot(final, mix_ref[n]).astype(BF16) for n, _ in chunks]
    mixed = [
        (latent_ref[n].astype(F32) + pulled[n].astype(F32)).astype(BF16) for n, _ in chunks
    ]
    decoded = [silu(dot(dec1_ref[...], mixed[n])).astype(BF16) for n, _ in chunks]
    for n, o in chunks:
        result = dot(dec2_ref[...], decoded[n]).astype(BF16)
        for r in range(step):
            out_ref[o + r] = result[:, r * cap : (r + 1) * cap]


TAIL_KINDS = "SSVV" + "V" * 12 + "HH"


def tail_scratch(nodes, width, hidden):
    return (
        pltpu.VMEM((2 * nodes, width), BF16),
        pltpu.VMEM((2 * nodes // BLK, width, BLK), BF16),
        pltpu.VMEM((width, nodes), BF16),
        pltpu.VMEM((hidden, nodes), BF16),
    )


def return_kernel(peers, cap, got, rank, owner, out):
    channels, grid = out.near.shape
    placed = rank_onehot(rank()[...], cap)
    chosen = owner_onehot(owner()[...], peers)
    total = jnp.zeros((channels, grid), F32)
    for o in range(peers):
        total = total + dot(got()[o], placed) * chosen[o : o + 1, :]
    out.near[...] = total.astype(BF16)


def body(
    grid_in,
    mesh_state,
    enc_owner,
    enc_slot,
    dec_owner,
    dec_slot,
    dec_weight,
    att_list,
    w_embed,
    w_message,
    norm_gain,
    w_qkv,
    w_out,
    w_up,
    w_down,
    w_dec1,
    w_dec2,
):
    peers = lax.axis_size("band")
    place = lax.axis_index("band")
    grid = grid_in.shape[0]
    nodes, width = mesh_state.shape
    cap = 2 * grid // peers
    channels = w_dec2.shape[1]
    slots = peers * cap

    def exchange(x):
        return lax.all_to_all(x, "band", split_axis=0, concat_axis=0, tiled=True)

    (enc_send,) = bucket(enc_owner.T, enc_slot.T, None, grid_in, (), peers, cap)
    enc_got = exchange(enc_send)
    dec_send, rank, key_w, embed_t, dec1_t, value_t, out_t, up_t, down_t = bucket(
        dec_owner.T,
        dec_slot.T,
        dec_weight.T,
        grid_in,
        (
            (w_embed, width),
            (w_dec1, width),
            (w_qkv[0], width),
            (w_out[0], width),
            (w_up[0], w_up.shape[2]),
            (w_down[0], width),
        ),
        peers,
        cap,
    )
    dec_got = exchange(dec_send)

    stream, normed = call(
        functools.partial(encode_kernel, peers, cap),
        (((nodes, width), F32, "H"), ((nodes, width), BF16, "H")),
        (enc_got, w_embed, w_message, mesh_state, norm_gain),
        "VHHHH",
        scratch=(pltpu.VMEM((nodes, slots), BF16), pltpu.VMEM((slots, width), BF16)),
        flops=2 * slots * width * (grid_in.shape[1] + width + nodes),
        moved=2 * slots * grid_in.shape[1] + 8 * nodes * width,
    )
    up = [(i, i + 1) for i in range(peers - 1)]
    down = [(j, i) for i, j in up]
    before = lax.ppermute(normed, "band", up)
    after = lax.ppermute(normed, "band", down)
    query_t, partial_t, stats, stream_t = call(
        local_kernel,
        (
            ((width, nodes), BF16, "H"),
            ((width, nodes), F32, "H"),
            ((2 * HEADS, nodes), F32, "H"),
            ((width, nodes), F32, "H"),
        ),
        (normed, w_qkv[0], value_t, stream),
        "HHHH",
        flops=2 * nodes * width * (3 * width + 2 * nodes),
        moved=2 * nodes * width * 8,
    )
    where = jnp.stack([place, jnp.int32(peers)]).astype(jnp.int32)
    carried = (
        key_w,
        value_t,
        query_t,
        stats,
        partial_t,
        stream_t,
        out_t,
        up_t,
        down_t,
        dec1_t,
    )
    many = (slots // ROWS, width, ROWS)
    near = call(
        functools.partial(request_kernel, peers, cap),
        [((slots // ROWS, nodes, ROWS), BF16, "V"), (many, BF16, "V")]
        + [(x.shape, x.dtype, "V") for x in carried],
        (dec_got, embed_t) + carried,
        "VH" + "R" * len(carried),
        scratch=(pltpu.SemaphoreType.DMA((len(carried),)),),
        flops=2 * slots * width * grid_in.shape[1],
        moved=24 * nodes * width,
    )
    (result,) = call(
        functools.partial(tail_kernel, peers, cap),
        (((peers, channels, cap), BF16, "V"),),
        (where, att_list, before, after, *near, norm_gain.T, w_dec2.T),
        TAIL_KINDS,
        scratch=tail_scratch(nodes, width, w_up.shape[2]),
        flops=2 * nodes * width * (4 * width + 2 * nodes + width + 2 * w_up.shape[2])
        + 2 * slots * width * (grid_in.shape[1] + nodes + width + 128),
        moved=2 * width * (3 * width + width + 2 * w_up.shape[2]) + 10 * nodes * width,
    )
    returned = exchange(result)
    (denoised,) = call(
        functools.partial(return_kernel, peers, cap),
        (((channels, grid), BF16, "V"),),
        (returned, rank, dec_owner.T),
        "VVV",
        flops=2 * slots * channels * grid,
        moved=2 * slots * channels,
    )
    return denoised


def solution(mesh):
    return jax.shard_map(
        body,
        mesh=mesh,
        in_specs=(
            P(("ens", "band"), None),
            P("band", None),
            P("band", None),
            P("band", None),
            P("band", None),
            P("band", None),
            P("band", None),
            P("band", None),
            P(),
            P(),
            P(),
            P(),
            P(),
            P(),
            P(),
            P(),
            P(),
        ),
        out_specs=P(None, ("ens", "band")),
        check_vma=False,
    )
```

```python
import functools

import jax
import jax.numpy as jnp
from jax import lax
from jax.experimental import pallas as pl
from jax.experimental.pallas import tpu as pltpu
from jax.sharding import PartitionSpec as P

HEADS = 4
BLK = 128
NB = 4
META = 8
ROWS = 512
LOW = 128
UPPER = 4
KEYS_OF = 2
MASKED = -1e30
LOG2E = 1.4426950408889634
PARTS = 4
VMEM_LIMIT = 24 * 1024 * 1024

epsilon = 1e-05

F32 = jnp.float32
BF16 = jnp.bfloat16


def dot(a, b):
    return jnp.dot(a, b, preferred_element_type=F32)


def dot_nt(a, b):
    return lax.dot_general(a, b, (((1,), (1,)), ((), ())), preferred_element_type=F32)


def silu(v):
    half = 0.5 * v
    return half + half * jnp.tanh(half)


def layer_norm(values, gains):
    average = jnp.mean(values, axis=-1, keepdims=True)
    centred = values - average
    spread_sq = jnp.mean(centred * centred, axis=-1, keepdims=True)
    return centred * lax.rsqrt(spread_sq + epsilon) * gains


class Held:
    def __init__(self, far, near, sem):
        self.near = near
        self.copy = pltpu.make_async_copy(far, near, sem)
        self.state = 0

    def start(self):
        if self.state == 0:
            self.copy.start()
            self.state = 1

    def __call__(self):
        self.start()
        if self.state == 1:
            self.copy.wait()
            self.state = 2
        return self.near


class Near:
    def __init__(self, ref):
        self.near = ref

    def __call__(self):
        return self.near

    def send(self, n=0, part=None):
        pass


class Sent:
    def __init__(self, near, far, sem):
        self.near, self.far, self.sem = near, far, sem
        self.copies = []

    def send(self, n=0, part=None):
        near, far = (self.near, self.far) if part is None else (self.near.at[part], self.far.at[part])
        self.copies.append(pltpu.make_async_copy(near, far, self.sem.at[n]))
        self.copies[-1].start()

    def finish(self):
        for c in self.copies:
            c.wait()


def call(kernel, outs, args, kinds, scratch=(), late=(), flops=0, moved=0):
    n_in, n_out = len(args), len(outs)
    far_in = [i for i in range(n_in) if kinds[i] == "H"]
    far_out = [i for i in range(n_out) if outs[i][2] == "H"]

    def wrapped(*refs):
        ins, results = refs[:n_in], refs[n_in : n_in + n_out]
        rest = list(refs[n_in + n_out :])
        sems, out_sems = rest.pop(0), rest.pop(0)
        ins = [Near(r) if kinds[i] == "V" else r for i, r in enumerate(ins)]
        results = [Near(r) for r in results]
        for n, i in enumerate(far_in):
            ins[i] = Held(refs[i], rest.pop(0), sems.at[n])
            if i not in late:
                ins[i].start()
        for n, i in enumerate(far_out):
            results[i] = Sent(rest.pop(0), refs[n_in + i], out_sems.at[n])
        kernel(*ins, *results, *rest)
        for i in far_in:
            ins[i]()
        for i in far_out:
            if not results[i].copies:
                results[i].send()
        for i in far_out:
            results[i].finish()

    spaces = {"V": pltpu.VMEM, "H": pltpu.HBM, "R": pltpu.HBM, "S": pltpu.SMEM}

    def spec(kind):
        return pl.BlockSpec(memory_space=pl.ANY if kind in "HR" else spaces[kind])

    def placed(x, kind):
        return x if kind == "S" else pltpu.with_memory_space_constraint(x, spaces[kind])

    return pl.pallas_call(
        wrapped,
        out_shape=tuple(
            pltpu.HBM(shape, dtype) if kind == "H" else jax.ShapeDtypeStruct(shape, dtype)
            for shape, dtype, kind in outs
        ),
        in_specs=[spec(kind) for kind in kinds],
        out_specs=tuple(spec(kind) for _, _, kind in outs),
        scratch_shapes=[
            pltpu.SemaphoreType.DMA((max(1, len(far_in)),)),
            pltpu.SemaphoreType.DMA((max(1, len(far_out)), PARTS)),
        ]
        + [pltpu.VMEM(args[i].shape, args[i].dtype) for i in far_in]
        + [pltpu.VMEM(outs[i][0], outs[i][1]) for i in far_out]
        + list(scratch),
        compiler_params=pltpu.CompilerParams(vmem_limit_bytes=VMEM_LIMIT),
        cost_estimate=pl.CostEstimate(flops=flops, bytes_accessed=moved, transcendentals=0),
    )(*[placed(x, kind) for x, kind in zip(args, kinds)])


def owner_onehot(owner, peers):
    places = lax.broadcasted_iota(jnp.int32, (peers, owner.shape[1]), 0)
    return jnp.where(places == owner, 1.0, 0.0).astype(F32)


def rank_onehot(rank, cap):
    places = lax.broadcasted_iota(jnp.int32, (cap, rank.shape[1]), 0).astype(F32)
    return jnp.where(places == rank, 1.0, 0.0).astype(BF16)


def bucket_kernel(peers, cap, weighted, turned, *refs):
    refs = list(refs)
    held_owner, held_slot = refs.pop(0), refs.pop(0)
    held_weight = refs.pop(0) if weighted else None
    held_rows = refs.pop(0)
    turns = [refs.pop(0) for _ in range(turned)]
    out = refs.pop(0)
    rank_out, key_out = (refs.pop(0), refs.pop(0)) if weighted else (None, None)
    turned_outs = [refs.pop(0) for _ in range(turned)]
    send_ref = out.near
    grid, width = held_rows.near.shape
    part = 256 if grid % 256 == 0 else grid
    upto = jnp.where(
        lax.broadcasted_iota(jnp.int32, (part, part), 0)
        <= lax.broadcasted_iota(jnp.int32, (part, part), 1),
        1.0,
        0.0,
    ).astype(BF16)
    owner = held_owner()[...]
    chosen = owner_onehot(owner, peers)
    chosen16 = chosen.astype(BF16)
    carry = jnp.zeros((peers, 1), F32)
    ranks = []
    for c in range(grid // part):
        span = slice(c * part, (c + 1) * part)
        counts = dot(chosen16[:, span], upto) + carry
        carry = counts[:, part - 1 :]
        ranks.append(jnp.sum(chosen[:, span] * counts, axis=0, keepdims=True) - 1.0)
    rank = jnp.concatenate(ranks, axis=1)
    if weighted:
        rank_out.near[...] = rank
    placed = rank_onehot(rank, cap)

    slots = held_slot()[...]
    lower = lax.rem(slots, LOW)
    upper = lax.div(slots, LOW)
    packed = upper[0:1]
    for k in range(1, slots.shape[0]):
        packed = packed + upper[k : k + 1] * UPPER**k
    pieces = [lower.astype(F32), packed.astype(F32)]
    if weighted:
        pieces.append(held_weight()[...])
    used = sum(p.shape[0] for p in pieces)
    if used < META:
        pieces.append(jnp.zeros((META - used, grid), F32))
    features = jnp.concatenate(pieces, axis=0).astype(BF16).astype(F32)
    spread = (chosen[:, None, :] * features[None, :, :]).reshape(peers * META, grid)
    meta = dot_nt(spread.astype(BF16), placed).reshape(peers, META, cap)
    send_ref[:, cap:, :] = jnp.zeros((peers, META, width), BF16)
    send_ref[:, cap:, :cap] = meta.astype(BF16)

    rows = held_rows()[...]
    step = ROWS // cap
    for n, o in enumerate(range(0, peers, step)):
        select = (chosen16[o : o + step, None, :] * placed[None, :, :]).reshape(step * cap, grid)
        moved = dot(select, rows)
        send_ref[o : o + step, :cap, :] = moved.astype(BF16).reshape(step, cap, width)
        out.send(n, pl.ds(o, step))
    for f, t in zip(turns, turned_outs):
        source = f()
        skipped = source.shape[1] - t.near.shape[0]
        t.near[...] = source[:, skipped:].T
        t.send()
    if weighted:
        columns = key_out.near.shape[1]
        key_out.near[...] = turns[KEYS_OF]()[:, columns : 2 * columns]


def bucket(owner, slots, weights, rows, turns, peers, cap):
    grid, width = rows.shape
    weighted = weights is not None
    args = (owner, slots) + ((weights,) if weighted else ()) + (rows,) + tuple(x for x, _ in turns)
    outs = [((peers, cap + META, width), BF16, "V")]
    if weighted:
        depth, columns = turns[KEYS_OF][0].shape
        outs += [((1, grid), F32, "H"), ((depth, columns // 3), BF16, "H")]
    outs += [((count, x.shape[0]), x.dtype, "H") for x, count in turns]
    return call(
        functools.partial(bucket_kernel, peers, cap, weighted, len(turns)),
        outs,
        args,
        "H" * len(args),
        flops=2 * peers * cap * grid * width,
        moved=2 * (grid * width + peers * (cap + META) * width),
    )


def meta_row(got_ref, o, step, cap, row):
    return jnp.concatenate(
        [got_ref[r, cap:, :cap].astype(F32)[row : row + 1, :] for r in range(o, o + step)],
        axis=1,
    )


def slot_rows(got_ref, o, step, cap, count):
    upper = meta_row(got_ref, o, step, cap, count).astype(jnp.int32)
    rows = []
    for k in range(count):
        rows.append(
            meta_row(got_ref, o, step, cap, k)
            + (lax.rem(lax.div(upper, UPPER**k), UPPER) * LOW).astype(F32)
        )
    return rows


def encode_kernel(peers, cap, got, embed, message_w, state, gain, stream, normed, target_ref, message_ref):
    got_ref = got()
    width = got_ref.shape[2]
    nodes = stream.near.shape[0]
    step = ROWS // cap
    places = lax.broadcasted_iota(jnp.int32, (nodes, ROWS), 0).astype(F32)
    starts = range(0, peers, step)
    for n, o in enumerate(starts):
        (slot,) = slot_rows(got_ref, o, step, cap, 1)
        target_ref[:, n * ROWS : (n + 1) * ROWS] = jnp.where(places == slot, 1.0, 0.0).astype(BF16)
    embed_ref = embed()
    latents = [
        silu(dot(got_ref[o : o + step, :cap, :].reshape(ROWS, width), embed_ref[...])).astype(BF16)
        for o in starts
    ]
    message_w_ref = message_w()
    for n, latent in enumerate(latents):
        message_ref[n * ROWS : (n + 1) * ROWS, :] = dot(latent, message_w_ref[...]).astype(BF16)
    total = state()[...].astype(F32) + dot(target_ref[...], message_ref[...])
    stream.near[...] = total
    stream.send()
    normed.near[...] = layer_norm(total, gain()[0:1, :]).astype(BF16)


def layer_norm_columns(values, gains):
    average = jnp.mean(values, axis=0, keepdims=True)
    centred = values - average
    spread_sq = jnp.mean(centred * centred, axis=0, keepdims=True)
    return centred * lax.rsqrt(spread_sq + epsilon) * gains


def local_kernel(normed, qkv, value_t, stream, query_t, partial_t, stats, stream_t):
    width, nodes = query_t.near.shape
    head = width // HEADS
    rate = head ** (-0.5) * LOG2E
    held = normed()[...]
    qkv_ref = qkv()
    queries = dot(held, qkv_ref[:, :width]).astype(BF16).T
    query_t.near[...] = queries
    query_t.send()
    key = dot(held, qkv_ref[:, width : 2 * width]).astype(BF16)
    value = dot_nt(value_t()[...], held).astype(BF16)
    for h in range(HEADS):
        rows = slice(h * head, (h + 1) * head)
        scores = dot(key[:, rows], queries[rows, :])
        highest = jnp.max(scores, axis=0, keepdims=True)
        probs = jnp.exp2((scores - highest) * rate)
        stats.near[h : h + 1, :] = highest
        stats.near[HEADS + h : HEADS + h + 1, :] = jnp.sum(probs, axis=0, keepdims=True)
        partial_t.near[rows, :] = dot(value[rows, :], probs.astype(BF16))
    stats.send()
    partial_t.send()
    stream_t.near[...] = stream()[...].T


def request_kernel(peers, cap, got, embed_t, *refs):
    carried = (len(refs) - 3) // 2
    sources, (mix, latent) = refs[:carried], refs[carried : carried + 2]
    targets, sems = refs[carried + 2 : -1], refs[-1]
    copies = [
        pltpu.make_async_copy(f, t.near, sems.at[n])
        for n, (f, t) in enumerate(zip(sources, targets))
    ]
    for c in copies:
        c.start()
    got_ref, mix_ref, latent_ref = got(), mix.near, latent.near
    nodes = mix_ref.shape[1]
    columns = got_ref.shape[2]
    step = ROWS // cap
    chunks = list(enumerate(range(0, peers, step)))

    places = lax.broadcasted_iota(jnp.int32, (nodes, ROWS), 0).astype(F32)
    for n, o in chunks:
        mix = jnp.zeros((nodes, ROWS), F32)
        for k, slot in enumerate(slot_rows(got_ref, o, step, cap, 3)):
            weight = meta_row(got_ref, o, step, cap, 4 + k)
            mix = mix + jnp.where(places == slot, weight, 0.0)
        mix_ref[n] = mix.astype(BF16)

    embed_ref = embed_t()
    for n, o in chunks:
        rows = got_ref[o : o + step, :cap, :].reshape(ROWS, columns)
        latent_ref[n] = silu(dot_nt(embed_ref[...], rows)).astype(BF16)
    for c in copies:
        c.wait()


def tail_kernel(
    peers,
    cap,
    where_ref,
    att_ref,
    before,
    after,
    mix,
    latent,
    key_w,
    value_t,
    query_t,
    stats,
    partial_t,
    stream_t,
    out_t,
    up_t,
    down_t,
    dec1_t,
    gain_t,
    dec2_t,
    out,
    key_ref,
    value_ref,
    attended_ref,
    hidden_ref,
):
    before_ref, after_ref, out_ref = before(), after(), out.near
    mix_ref, latent_ref = mix(), latent()
    width, nodes = attended_ref.shape
    head = width // HEADS
    blocks = nodes // BLK
    rate = head ** (-0.5) * LOG2E
    has_before = where_ref[0] > 0
    has_after = where_ref[0] < where_ref[1] - 1
    step = ROWS // cap
    chunks = list(enumerate(range(0, peers, step)))

    key_w_ref, value_t_ref = key_w(), value_t()
    for n, side in enumerate((before_ref, after_ref)):
        key_ref[n * nodes : (n + 1) * nodes, :] = dot(side[...], key_w_ref[...]).astype(
            BF16
        )
        value = dot_nt(value_t_ref[...], side[...]).astype(BF16)
        for i in range(blocks):
            value_ref[n * blocks + i] = value[:, i * BLK : (i + 1) * BLK]

    query_ref, stats_ref, partial_ref = query_t(), stats(), partial_t()
    named = [[att_ref[i, k] for k in range(NB)] for i in range(blocks)]
    starts = [[pl.multiple_of(w * BLK, BLK) for w in row] for row in named]
    allowed = [
        [jnp.where(jnp.where(w < blocks, has_before, has_after), 0.0, MASKED) for w in row]
        for row in named
    ]
    for h in range(HEADS):
        rows = slice(h * head, (h + 1) * head)
        scores = []
        for i in range(blocks):
            queries = query_ref[rows, i * BLK : (i + 1) * BLK]
            keys = jnp.concatenate([key_ref[pl.ds(s, BLK), rows] for s in starts[i]], axis=0)
            found = dot(keys, queries)
            scores.append(
                jnp.concatenate(
                    [found[k * BLK : (k + 1) * BLK] + allowed[i][k] for k in range(NB)], axis=0
                )
            )
        scores = jnp.concatenate(scores, axis=1)
        held = stats_ref[h : h + 1, :]
        highest = jnp.maximum(held, jnp.max(scores, axis=0, keepdims=True))
        probs = jnp.exp2((scores - highest) * rate)
        keep = jnp.exp2((held - highest) * rate)
        totals = stats_ref[HEADS + h : HEADS + h + 1, :] * keep + jnp.sum(
            probs, axis=0, keepdims=True
        )
        weights = probs.astype(BF16)
        remote = []
        for i in range(blocks):
            values = jnp.concatenate([value_ref[w, rows, :] for w in named[i]], axis=1)
            remote.append(dot(values, weights[:, i * BLK : (i + 1) * BLK]))
        combined = partial_ref[rows, :] * keep + jnp.concatenate(remote, axis=1)
        attended_ref[rows, :] = (combined / totals).astype(BF16)

    gains = gain_t()[...]
    stream = stream_t()[...] + dot(out_t()[...], attended_ref[...])
    normed = layer_norm_columns(stream, gains[:, 1:2]).astype(BF16)
    up_ref = up_t()
    for c in range(0, up_ref.shape[0], width):
        hidden_ref[c : c + width, :] = silu(dot(up_ref[c : c + width, :], normed)).astype(BF16)
    stream = stream + dot(down_t()[...], hidden_ref[...])
    final = layer_norm_columns(stream, gains[:, 2:3]).astype(BF16)

    dec1_ref, dec2_ref = dec1_t(), dec2_t()
    pulled = [dot(final, mix_ref[n]).astype(BF16) for n, _ in chunks]
    mixed = [
        (latent_ref[n].astype(F32) + pulled[n].astype(F32)).astype(BF16) for n, _ in chunks
    ]
    decoded = [silu(dot(dec1_ref[...], mixed[n])).astype(BF16) for n, _ in chunks]
    for n, o in chunks:
        result = dot(dec2_ref[...], decoded[n]).astype(BF16)
        for r in range(step):
            out_ref[o + r] = result[: out_ref.shape[1], r * cap : (r + 1) * cap]


TAIL_KINDS = "SSVV" + "V" * 12 + "HH"


def tail_scratch(nodes, width, hidden):
    return (
        pltpu.VMEM((2 * nodes, width), BF16),
        pltpu.VMEM((2 * nodes // BLK, width, BLK), BF16),
        pltpu.VMEM((width, nodes), BF16),
        pltpu.VMEM((hidden, nodes), BF16),
    )


def return_kernel(peers, cap, got, rank, owner, out):
    channels, grid = out.near.shape
    placed = rank_onehot(rank()[...], cap)
    chosen = owner_onehot(owner()[...], peers)
    total = jnp.zeros((channels, grid), F32)
    for o in range(peers):
        total = total + dot(got()[o], placed) * chosen[o : o + 1, :]
    out.near[...] = total.astype(BF16)


def body(
    grid_in,
    mesh_state,
    enc_owner,
    enc_slot,
    dec_owner,
    dec_slot,
    dec_weight,
    att_list,
    w_embed,
    w_message,
    norm_gain,
    w_qkv,
    w_out,
    w_up,
    w_down,
    w_dec1,
    w_dec2,
):
    peers = lax.axis_size("band")
    place = lax.axis_index("band")
    grid = grid_in.shape[0]
    nodes, width = mesh_state.shape
    cap = 2 * grid // peers
    channels = w_dec2.shape[1]
    slots = peers * cap

    def exchange(x):
        return lax.all_to_all(x, "band", split_axis=0, concat_axis=0, tiled=True)

    (enc_send,) = bucket(enc_owner.T, enc_slot.T, None, grid_in, (), peers, cap)
    enc_got = exchange(enc_send)
    dec_send, rank, key_w, embed_t, dec1_t, value_t, out_t, up_t, down_t = bucket(
        dec_owner.T,
        dec_slot.T,
        dec_weight.T,
        grid_in,
        (
            (w_embed, width),
            (w_dec1, width),
            (w_qkv[0], width),
            (w_out[0], width),
            (w_up[0], w_up.shape[2]),
            (w_down[0], width),
        ),
        peers,
        cap,
    )
    dec_got = exchange(dec_send)

    stream, normed = call(
        functools.partial(encode_kernel, peers, cap),
        (((nodes, width), F32, "H"), ((nodes, width), BF16, "H")),
        (enc_got, w_embed, w_message, mesh_state, norm_gain),
        "VHHHH",
        scratch=(pltpu.VMEM((nodes, slots), BF16), pltpu.VMEM((slots, width), BF16)),
        flops=2 * slots * width * (grid_in.shape[1] + width + nodes),
        moved=2 * slots * grid_in.shape[1] + 8 * nodes * width,
    )
    up = [(i, i + 1) for i in range(peers - 1)]
    down = [(j, i) for i, j in up]
    before = lax.ppermute(normed, "band", up)
    after = lax.ppermute(normed, "band", down)
    query_t, partial_t, stats, stream_t = call(
        local_kernel,
        (
            ((width, nodes), BF16, "H"),
            ((width, nodes), F32, "H"),
            ((2 * HEADS, nodes), F32, "H"),
            ((width, nodes), F32, "H"),
        ),
        (normed, w_qkv[0], value_t, stream),
        "HHHH",
        flops=2 * nodes * width * (3 * width + 2 * nodes),
        moved=2 * nodes * width * 8,
    )
    where = jnp.stack([place, jnp.int32(peers)]).astype(jnp.int32)
    carried = (
        key_w,
        value_t,
        query_t,
        stats,
        partial_t,
        stream_t,
        out_t,
        up_t,
        down_t,
        dec1_t,
    )
    dec2_t = jnp.pad(w_dec2.T, ((0, -channels % 16), (0, 0)))
    many = (slots // ROWS, width, ROWS)
    near = call(
        functools.partial(request_kernel, peers, cap),
        [((slots // ROWS, nodes, ROWS), BF16, "V"), (many, BF16, "V")]
        + [(x.shape, x.dtype, "V") for x in carried],
        (dec_got, embed_t) + carried,
        "VH" + "R" * len(carried),
        scratch=(pltpu.SemaphoreType.DMA((len(carried),)),),
        flops=2 * slots * width * grid_in.shape[1],
        moved=24 * nodes * width,
    )
    (result,) = call(
        functools.partial(tail_kernel, peers, cap),
        (((peers, channels, cap), BF16, "V"),),
        (where, att_list, before, after, *near, norm_gain.T, dec2_t),
        TAIL_KINDS,
        scratch=tail_scratch(nodes, width, w_up.shape[2]),
        flops=2 * nodes * width * (4 * width + 2 * nodes + width + 2 * w_up.shape[2])
        + 2 * slots * width * (grid_in.shape[1] + nodes + width + 128),
        moved=2 * width * (3 * width + width + 2 * w_up.shape[2]) + 10 * nodes * width,
    )
    returned = exchange(result)
    (denoised,) = call(
        functools.partial(return_kernel, peers, cap),
        (((channels, grid), BF16, "V"),),
        (returned, rank, dec_owner.T),
        "VVV",
        flops=2 * slots * channels * grid,
        moved=2 * slots * channels,
    )
    return denoised


def solution(mesh):
    return jax.shard_map(
        body,
        mesh=mesh,
        in_specs=(
            P(("ens", "band"), None),
            P("band", None),
            P("band", None),
            P("band", None),
            P("band", None),
            P("band", None),
            P("band", None),
            P("band", None),
            P(),
            P(),
            P(),
            P(),
            P(),
            P(),
            P(),
            P(),
            P(),
        ),
        out_specs=P(None, ("ens", "band")),
        check_vma=False,
    )
```
